32 devices in a mesh: sub: 16 (over z, y, x), panel: 2 (over core).
Axes of the slice: x: 2, y: 2, z: 4, core: 2. Of those that a mesh axis runs over, the one named last changes fastest.
Arguments:
- stiffness_tiles: bfloat16 [256, 8, 128, 128], P('sub'), may hold values from -0.1875 to 0.1875
- tile_columns: int32 [256, 8], P('sub'), may hold values from 0 to 19
- tile_counts: int32 [16, 16], P('sub'), may hold values from 1 to 8, 96 in all within a row
- phi_modes: bfloat16 [32768, 2048], P('sub', 'panel'), may hold values from -1.5 to 1.5
- halo_to_right: int32 [32], P('sub'), may hold values from 0 to 15
- halo_to_left: int32 [32], P('sub'), may hold values from 0 to 15
- liner_rows: int32 [8192], P('sub'), may hold values from 0 to 2047
- liner_owner: int32 [8192, 1], P('sub'), may hold values from 0 to 15; in each aligned block of 512 rows (0 to 511, 512 to 1023, ...) at most 32 rows name the same one
- liner_slot: int32 [8192], P('sub'), may hold values from 0 to 31
Outputs:
- reduced: float32 [2048, 2048], P('sub', 'panel')
- interface_load: float32 [512, 2048], P('sub', 'panel')
The draws below stay inside these ranges and needn't reach their ends.
Inputs may be any that keep to these rules, and one draw needn't show every extreme that they name: `tile_counts`: counts a slab's used slots; the counts of one slab sum to 96. `tile_columns`: indices into the slab's extended tiles. `liner_owner`: among the listed rows of one slab at most 32 name one owner, and in every draw some owner is named by exactly 32 rows of some slab.
All inputs are finite; a program needn't handle non-finite values.
Results may differ from the reference program's by a relative error of at most 0.0029.
Values may be sent and summed in bfloat16 or wider, within the bound.
A program may use at most 128 MiB of HBM per device.

```python
import math
import jax
import jax.numpy as jnp
import numpy as np
from jax import lax

MODES = 2048
TILE = 128
NNZ = 8
NBR = 16
HALO_T = 2
SEND_DEV = 512
CAP = 32
IF_DEV = 32
ROWS = 2048
DOFS = 32768
N_SUB = 16


def with_ends(result, stream_key, low, largest):
    index_at = [jax.random.randint(jax.random.fold_in(stream_key, axis), (), 0, length) for axis, length in enumerate(result.shape)]
    widest = result.shape.index(max(result.shape))
    beside = index_at[:widest] + [(index_at[widest] + 1) % result.shape[widest]] + index_at[widest + 1:]
    return result.at[tuple(index_at)].set(low).at[tuple(beside)].set(largest)


def with_spikes(values, key, source, target, blocks, factor):
    owner, partner = [(jnp.arange(values.shape[position]) // (values.shape[position] // blocks)).reshape([-1 if axis == position else 1 for axis in range(values.ndim)]) for position in (source, target)]
    chosen = jax.random.permutation(key, blocks)[partner]
    strong = (owner == chosen) | (owner == (partner + blocks // 2) % blocks)
    return jnp.where(strong, factor * values, values)


def block_scale(stream_key, dims, cuts, low, high):
    factor_of, own = 1.0, jax.random.fold_in(stream_key, 6)
    for dim, parts in cuts:
        steps = jnp.exp(jax.random.uniform(jax.random.fold_in(own, dim), (parts,), jnp.float32, low / len(cuts), high / len(cuts)))
        factor_of = factor_of * jnp.repeat(steps, dims[dim] // parts).reshape([-1 if axis == dim else 1 for axis in range(len(dims))])
    return factor_of


def split_up(number_of, total, bound, lean):
    loads = [(1 << 20) // math.isqrt(standing ** lean) + 1 for standing in range(2, number_of + 1)]
    rest, given = total - bound - (number_of - 1), [1] * (number_of - 1)
    while rest > 0:
        free = [i for i in range(number_of - 1) if given[i] < bound]
        mass, budget = sum([loads[i] for i in free]), rest
        for i in free:
            more = min(bound - given[i], max(1, budget * loads[i] // mass), rest)
            given[i] = given[i] + more
            rest = rest - more
    return np.array([bound] + given)


def uneven_parts(key, count, total, limit, skew):
    if count == 2:
        one = jax.random.randint(key, (), max(1, total - limit), min(limit, total - 1) + 1)
        return jnp.stack([one, total - one])
    sizes = jnp.asarray(split_up(count, total, limit, skew), jnp.int32)
    couples = (count - 1) // 2
    giver, sink = sizes[1:1 + 2 * couples:2], sizes[2:2 + 2 * couples:2]
    room = jnp.minimum(giver - 1, limit - sink)
    moved = jax.random.randint(jax.random.fold_in(key, 1), (couples,), 0, 1 << 20) % (room + 1)
    sizes = sizes.at[1:1 + 2 * couples:2].set(giver - moved).at[2:2 + 2 * couples:2].set(sink + moved)
    return sizes[jax.random.permutation(jax.random.fold_in(key, 2), count)]


def shared_out(own_key, own, number, rows, amount, top, bound, lean):
    ranking = jax.random.permutation(own_key, amount)
    crowded, usual = shares(amount, rows * top, bound, lean, True), shares(amount, rows * top, bound, lean, False)
    places = jnp.arange(amount)

    def named(tallies, turn):
        used = int((tallies > 0).sum())
        fixed = max(1, used // 4)
        moved = fixed + (places - fixed + turn * (used - fixed)) % max(1, amount - fixed)
        return jnp.zeros((amount,), jnp.int32).at[ranking[jnp.where(places < fixed, places, moved)]].set(jnp.asarray(tallies, jnp.int32))

    tallies = jnp.where(number % 4 == 0, named(crowded, number // 4), named(usual, number - number // 4 - 1))
    mixed = jax.random.permutation(jax.random.fold_in(own, 3), amount)
    giver, receiver = mixed[0:amount // 2 * 2:2], mixed[1:amount // 2 * 2:2]
    room = jnp.minimum(tallies[giver] - 1, bound - tallies[receiver]) // 2
    room = jnp.where((giver == ranking[0]) | (receiver == ranking[0]) | (tallies[receiver] == 0), 0, jnp.maximum(room, 0))
    moved = jax.random.randint(jax.random.fold_in(own, 4), (amount // 2,), 0, 1 << 20) % (room + 1)
    tallies = tallies.at[giver].add(-moved).at[receiver].add(moved)
    labels = jnp.searchsorted(jnp.cumsum(tallies), jnp.arange(rows * top), side="right").astype(jnp.int32)
    table = labels.reshape(top, rows).T
    table = table[jax.random.permutation(jax.random.fold_in(own, 1), rows)]
    turn = jax.random.randint(jax.random.fold_in(own, 2), (rows, 1), 0, top)
    return jnp.take_along_axis(table, (jnp.arange(top)[None, :] + turn) % top, axis=1)


def shares(number_of, total, bound, slope, full):
    loads = [(1 << 20) // math.isqrt(standing ** slope) + 1 for standing in range(1, number_of + 1)]
    largest = bound if full else min(bound, max(-(-total // number_of), total * loads[0] // sum(loads)))
    least = 1 if total - largest >= number_of - 1 else 0
    given, spare = [largest] + [least] * (number_of - 1), total - largest - least * (number_of - 1)
    while spare > 0:
        movable = [i for i in range(1, number_of) if given[i] < largest] or [i for i in range(1, number_of) if given[i] < bound]
        pool, left = sum([loads[i] for i in movable]), spare
        for i in movable:
            more = min(bound - given[i], max(1, left * loads[i] // pool), spare)
            given[i] = given[i] + more
            spare = spare - more
    return np.array(given)


def centred(rng, dims, deviation, limit, pieces=(), kind=jnp.bfloat16):
    factor_of = block_scale(rng, dims, pieces, -0.22, 0.18) if pieces else 1.0
    array = jax.random.normal(rng, dims, jnp.float32) * deviation * factor_of
    return jnp.minimum(jnp.maximum(array, -limit), limit).astype(kind)


def noise_with(key, dims, scale, most, split, heavy, kind=jnp.bfloat16):
    entries = scale * jax.random.normal(key, dims, jnp.float32)
    if split:
        entries = entries * block_scale(key, dims, split, -0.22, 0.18)
    return jnp.clip(with_spikes(entries, jax.random.fold_in(key, 3), *heavy), -most, most).astype(kind)


def setup_inputs(seed: int = 0) -> dict:
    keys = jax.random.split(jax.random.key(seed), 10)
    stiffness_tiles = centred(keys[0], (N_SUB * NBR, NNZ, TILE, TILE), (NNZ * TILE) ** -0.5, 0.1875, ((0, 16),))
    tile_columns = with_ends(jax.random.randint(keys[1], (N_SUB * NBR, NNZ), 0, NBR + 2 * HALO_T), jax.random.fold_in(keys[1], 1), 0, (NBR + 2 * HALO_T) - 1).astype(jnp.int32)
    tile_counts = jax.vmap(lambda own: uneven_parts(own, NBR, NBR * NNZ * 3 // 4, NNZ, 2))(jax.random.split(keys[2], N_SUB)).reshape((N_SUB, NBR)).astype(jnp.int32)
    phi_modes = noise_with(keys[3], (DOFS, MODES), (DOFS ** -0.25), 1.5, ((0, 16), (1, 2)), (0, 1, 16, 2.0))
    halo_to_right = with_ends(jax.random.randint(keys[4], (N_SUB * HALO_T,), 0, NBR), jax.random.fold_in(keys[4], 1), 0, NBR - 1).astype(jnp.int32)
    halo_to_left = with_ends(jax.random.randint(keys[5], (N_SUB * HALO_T,), 0, NBR), jax.random.fold_in(keys[5], 1), 0, NBR - 1).astype(jnp.int32)
    liner_rows = with_ends(jax.random.randint(keys[6], (N_SUB * SEND_DEV,), 0, ROWS), jax.random.fold_in(keys[6], 1), 0, ROWS - 1).astype(jnp.int32)
    liner_owner_keys = jax.random.split(jax.random.fold_in(keys[7], 1), (N_SUB * SEND_DEV) // SEND_DEV)
    liner_owner_turns = jax.random.permutation(jax.random.fold_in(keys[7], 3), (N_SUB * SEND_DEV) // SEND_DEV)
    liner_owner = jax.vmap(lambda own, number: shared_out(jax.random.fold_in(keys[7], 2), own, number, SEND_DEV, N_SUB, 1, CAP, 2))(liner_owner_keys, liner_owner_turns).reshape((N_SUB * SEND_DEV, 1))
    liner_slot = with_ends(jax.random.randint(keys[8], (N_SUB * SEND_DEV,), 0, IF_DEV), jax.random.fold_in(keys[8], 1), 0, IF_DEV - 1).astype(jnp.int32)
    return {"stiffness_tiles": stiffness_tiles, "tile_columns": tile_columns, "tile_counts": tile_counts, "phi_modes": phi_modes, "halo_to_right": halo_to_right, "halo_to_left": halo_to_left, "liner_rows": liner_rows, "liner_owner": liner_owner, "liner_slot": liner_slot}


def slab_product(packed):
    tiles_here, columns_here, counts_here, extended = packed
    slots = jnp.arange(NNZ, dtype=jnp.int32)
    usable = (slots[None, :] < counts_here[:, None]).astype(jnp.bfloat16)
    masked = tiles_here * usable[:, :, None, None]
    chosen = extended[columns_here]
    return jnp.einsum("bjrc,bjcm->brm", masked.astype(jnp.float32), chosen.astype(jnp.float32))


def reference(stiffness_tiles, tile_columns, tile_counts, phi_modes, halo_to_right, halo_to_left, liner_rows, liner_owner, liner_slot):
    phi_tiles = phi_modes.reshape(N_SUB, NBR, TILE, MODES)
    right_lists = halo_to_right.reshape(N_SUB, HALO_T)
    left_lists = halo_to_left.reshape(N_SUB, HALO_T)
    picker = jax.vmap(lambda group, listed: group[listed])
    sent_right = picker(phi_tiles, right_lists)
    sent_left = picker(phi_tiles, left_lists)
    blanks = jnp.zeros((1, HALO_T, TILE, MODES), jnp.bfloat16)
    left_halo = jnp.concatenate([blanks, sent_right[:-1]], axis=0)
    right_halo = jnp.concatenate([sent_left[1:], blanks], axis=0)
    extended = jnp.concatenate([left_halo, phi_tiles, right_halo], axis=1)
    kphi = lax.map(slab_product, (stiffness_tiles.reshape(N_SUB, NBR, NNZ, TILE, TILE), tile_columns.reshape(N_SUB, NBR, NNZ), tile_counts, extended))
    kphi = kphi.astype(jnp.bfloat16).reshape(N_SUB * ROWS, MODES)
    reduced = jnp.dot(phi_modes.T, kphi, preferred_element_type=jnp.float32)
    source = (jnp.arange(N_SUB * SEND_DEV, dtype=jnp.int32) // SEND_DEV) * ROWS + liner_rows
    values = kphi[source].astype(jnp.float32)
    target = liner_owner[:, 0] * IF_DEV + liner_slot
    interface_load = jax.ops.segment_sum(values, target, num_segments=N_SUB * IF_DEV)
    return reduced, interface_load
```

```python
import functools

import jax
import jax.numpy as jnp
from jax import lax
from jax.experimental import pallas as pl
from jax.experimental.pallas import tpu as pltpu
from jax.sharding import PartitionSpec as P

IF_DEV = 32
LOW = 4
LAG = 3
CHAIN_LAG = 1
CHAIN_ROWS = 48
LONGEST_CHAIN = 4
MESH = pl.DeviceIdType.MESH


def sizes(n_sub, width, mode_rows):
    parts = max(1, min(4, width // 128))
    high = n_sub // LOW
    chain = CHAIN_ROWS if high <= LONGEST_CHAIN and mode_rows % 16 == 0 else 0
    return parts, width // parts, high, chain


def kernel(n_sub, n_panel, parts, chain, *refs):
    refs = list(refs)

    def take(count):
        taken, refs[:] = refs[:count], refs[count:]
        return taken

    cols_ref, counts_ref, to_right_ref, to_left_ref, rows_ref, owner_ref, slot_ref = take(7)
    tiles_hbm, phi_hbm, red_ref, load_ref = take(4)
    ext = take(parts)
    tiles, onehot, lhs, kphi, part, halo_out, halo_in = take(7)
    s1_out, s1_in, s2_out, s2_in, z_out, z_in = take(6)
    c_out, c_in, c1_out, c1_in, c2_out, c2_in = take(6)
    local_sem, halo_send, halo_recv, pan_send, pan_recv = take(5)
    s1_send, s1_recv, s2_send, s2_recv, z_send, z_recv = take(6)
    c_send, c_recv, c1_send, c1_recv, c2_send, c2_recv = take(6)

    block_rows, slots, tile, _ = tiles.shape
    halo = halo_out.shape[2]
    rows = block_rows * tile
    width = kphi.shape[2]
    high = n_sub // LOW
    mode_rows = red_ref.shape[0]
    out_rows = mode_rows + IF_DEV
    direct = out_rows - chain
    per_panel = high // n_panel
    total_steps = parts * high
    empty = block_rows + 2 * halo
    f32, bf16 = jnp.float32, jnp.bfloat16
    sub = lax.axis_index("sub")
    panel = lax.axis_index("panel")
    low, my_high = lax.rem(sub, LOW), sub // LOW
    bit0, bit1 = lax.rem(low, 2), low // 2
    odd = lax.rem(panel, 2)

    def order(c):
        first0 = jnp.where(c == parts - 1, 1 - odd, 0) + jnp.where(c == parts - 2, odd, 0)
        swap = 1 - first0
        first_bit = (1 - swap) * bit0 + swap * bit1
        second_bit = (1 - swap) * bit1 + swap * bit0
        first_weight, second_weight = 1 + swap, 2 - swap
        first_peer = sub + (1 - 2 * first_bit) * first_weight
        second_peer = sub + (1 - 2 * second_bit) * second_weight
        return first_bit, second_bit, first_weight, second_weight, first_peer, second_peer

    below, above = my_high, high - 1 - my_high
    nearer = jnp.minimum(below, above)
    excess = jnp.abs(above - below)
    far_way = jnp.where(above >= below, 1, -1)

    def dest(t):
        k = lax.rem(t, high)
        own_first = lax.rem(k + panel * per_panel, high)
        later = jnp.maximum(k - excess, 0)
        distance = jnp.where(k < excess, nearer + excess - k, nearer - later // 2)
        way = jnp.where((k < excess) | (lax.rem(later, 2) == 0), far_way, -far_way)
        return jnp.where(t < high, own_first, my_high + way * distance)

    barrier = pltpu.get_barrier_semaphore()

    def greet(place):
        pl.semaphore_signal(barrier, inc=1, device_id=place, device_id_type=MESH)

    greet({"sub": sub + 1 - 2 * bit0, "panel": panel})
    greet({"sub": sub + 2 - 4 * bit1, "panel": panel})

    @pl.when(sub > 0)
    def _():
        greet({"sub": sub - 1, "panel": panel})

    @pl.when(sub < n_sub - 1)
    def _():
        greet({"sub": sub + 1, "panel": panel})

    for step in range(1, n_panel):
        greet({"sub": sub, "panel": lax.rem(panel + step, n_panel)})
    for step in range(1, high):
        greet({"sub": lax.rem(my_high + step, high) * LOW + low, "panel": panel})

    phi_copies = [
        pltpu.make_async_copy(
            phi_hbm.at[:, :, pl.ds(c * width, width)],
            ext[c].at[pl.ds(halo, block_rows)],
            local_sem.at[c],
        )
        for c in range(parts)
    ]
    tile_copy = pltpu.make_async_copy(tiles_hbm, tiles, local_sem.at[parts])
    for copy in phi_copies:
        copy.start()
    tile_copy.start()

    def halo_copy(c, side):
        return pltpu.make_async_remote_copy(
            src_ref=halo_out.at[c, side],
            dst_ref=halo_in.at[c, side],
            send_sem=halo_send.at[c, side],
            recv_sem=halo_recv.at[c, side],
            device_id={"sub": sub + 1 - 2 * side, "panel": panel},
            device_id_type=MESH,
        )

    def prepare_halo(c):
        phi_copies[c].wait()
        for i in range(halo):
            halo_out[c, 0, i] = ext[c][halo + to_right_ref[i]]
            halo_out[c, 1, i] = ext[c][halo + to_left_ref[i]]

    def send_halo(c):
        @pl.when(sub < n_sub - 1)
        def _():
            halo_copy(c, 0).start()

        @pl.when(sub > 0)
        def _():
            halo_copy(c, 1).start()

    prepare_halo(0)
    ends = jnp.where(sub > 0, 1, 0) + jnp.where(sub < n_sub - 1, 1, 0)
    pl.semaphore_wait(barrier, 2 + (n_panel - 1) + (high - 1) + ends)
    send_halo(0)
    for c in range(1, parts):
        prepare_halo(c)

    def panel_copy(step, piece, owner):
        block = lhs.at[owner * per_panel + piece, :, pl.ds(0, mode_rows), :]
        return pltpu.make_async_remote_copy(
            src_ref=block,
            dst_ref=block,
            send_sem=pan_send.at[step, piece],
            recv_sem=pan_recv.at[step, piece],
            device_id={"sub": sub, "panel": lax.rem(panel + step, n_panel)},
            device_id_type=MESH,
        )

    for piece in range(per_panel):

        def transposed(b, carry, piece=piece):
            for q in range(LOW):
                at = (piece * LOW + q) * mode_rows
                lhs[
                    panel * per_panel + piece,
                    q,
                    pl.ds(0, mode_rows),
                    pl.ds(pl.multiple_of(b * tile, tile), tile),
                ] = jnp.transpose(
                    ext[at // width][halo + b, :, pl.ds(at % width, mode_rows)]
                )
            return carry

        lax.fori_loop(0, block_rows, transposed, 0)
        for step in range(1, n_panel):
            panel_copy(step, piece, panel).start()

    listed = rows_ref.shape[1]
    onehot[...] = (
        (lax.broadcasted_iota(jnp.int32, (rows, listed), 0) == rows_ref[...])
        .astype(f32)
        .astype(bf16)
    )
    target = owner_ref[...] * IF_DEV + slot_ref[...]
    wanted = LOW * IF_DEV

    def select(h, carry):
        place = lax.broadcasted_iota(jnp.int32, (wanted, listed), 0) + h * wanted
        hit = (place == target).astype(f32).astype(bf16)
        found = lax.dot_general(
            hit,
            onehot[...],
            (((1,), (1,)), ((), ())),
            preferred_element_type=f32,
        ).astype(bf16)
        for q in range(LOW):
            lhs[h, q, pl.ds(mode_rows, IF_DEV), :] = found[
                q * IF_DEV : (q + 1) * IF_DEV
            ]
        return carry

    lax.fori_loop(0, high, select, 0)
    for c in range(parts):
        ext[c][empty] = jnp.zeros((tile, width), bf16)
    tile_copy.wait()

    def products(c):
        for side in range(2):
            there = sub > 0 if side == 0 else sub < n_sub - 1
            place = pl.ds(side * (halo + block_rows), halo)

            @pl.when(there)
            def _(side=side, place=place):
                halo_copy(c, side).wait_recv()
                ext[c][place] = halo_in[c, side]

            @pl.when(jnp.logical_not(there))
            def _(place=place):
                ext[c][place] = jnp.zeros((halo, tile, width), bf16)

        if c + 1 < parts:
            send_halo(c + 1)

        def block_row(b, carry):
            count = counts_ref[0, b]
            left = jnp.concatenate([tiles[b, j] for j in range(slots)], axis=1)
            right = jnp.concatenate(
                [
                    ext[c][jnp.where(j < count, cols_ref[j, b], empty)]
                    for j in range(slots)
                ],
                axis=0,
            )
            kphi[c, pl.ds(pl.multiple_of(b * tile, tile), tile), :] = jnp.dot(
                left, right, preferred_element_type=f32
            ).astype(bf16)
            return carry

        lax.fori_loop(0, block_rows, block_row, 0, unroll=4)

    def first_copy(k):
        return pltpu.make_async_remote_copy(
            src_ref=s1_out.at[k],
            dst_ref=s1_in.at[k],
            send_sem=s1_send.at[k],
            recv_sem=s1_recv.at[k],
            device_id={"sub": order(k // high)[4], "panel": panel},
            device_id_type=MESH,
        )

    def second_copy(k):
        return pltpu.make_async_remote_copy(
            src_ref=s2_out.at[k],
            dst_ref=s2_in.at[k],
            send_sem=s2_send.at[k],
            recv_sem=s2_recv.at[k],
            device_id={"sub": order(k // high)[5], "panel": panel},
            device_id_type=MESH,
        )

    def third_copy(k, h, slot):
        return pltpu.make_async_remote_copy(
            src_ref=z_out.at[k],
            dst_ref=z_in.at[slot],
            send_sem=z_send.at[k],
            recv_sem=z_recv.at[slot],
            device_id={"sub": h * LOW + low, "panel": panel},
            device_id_type=MESH,
        )

    def chain_copy(k, next_high, slot):
        return pltpu.make_async_remote_copy(
            src_ref=c_out.at[k],
            dst_ref=c_in.at[slot],
            send_sem=c_send.at[k],
            recv_sem=c_recv.at[slot],
            device_id={"sub": next_high * LOW + low, "panel": panel},
            device_id_type=MESH,
        )

    def chain_first(c):
        return pltpu.make_async_remote_copy(
            src_ref=c1_out.at[c],
            dst_ref=c1_in.at[c],
            send_sem=c1_send.at[c],
            recv_sem=c1_recv.at[c],
            device_id={"sub": order(c)[4], "panel": panel},
            device_id_type=MESH,
        )

    def chain_second(c):
        return pltpu.make_async_remote_copy(
            src_ref=c2_out.at[c],
            dst_ref=c2_in.at[c],
            send_sem=c2_send.at[c],
            recv_sem=c2_recv.at[c],
            device_id={"sub": order(c)[5], "panel": panel},
            device_id_type=MESH,
        )

    head, tail = pl.ds(0, direct), pl.ds(direct, chain)

    def chain_add(k, slot):
        chain_copy(k, my_high, slot).wait_recv()
        part[k, :, tail, :] += c_in[slot].astype(f32)

    def chain_step(k):
        h = dest(k)
        c = k // high
        base = c * (high + 1)

        @pl.when(h != my_high)
        def _():
            up = jnp.where(h > my_high, 1, 0)

            @pl.when(jnp.where(up == 1, below, above) > 0)
            def _():
                chain_add(k, base + h)

            c_out[k] = part[k, :, tail, :].astype(bf16)
            next_high = my_high + 2 * up - 1
            slot = jnp.where((up == 0) & (next_high == h), high, h)
            chain_copy(k, next_high, base + slot).start()

        @pl.when(h == my_high)
        def _():
            @pl.when(below > 0)
            def _():
                chain_add(k, base + my_high)

            @pl.when(above > 0)
            def _():
                chain_add(k, base + high)

            first_bit, _, first_weight, second_weight, _, _ = order(c)
            for j in range(2):
                q = (1 - first_bit) * first_weight + j * second_weight
                c1_out[c, j] = part[k, q, tail, :].astype(bf16)
            chain_first(c).start()

    def chain_turn(k):
        c = k // high
        first_bit, second_bit, first_weight, second_weight, _, _ = order(c)
        chain_first(c).wait_recv()
        q = first_bit * first_weight + (1 - second_bit) * second_weight
        c2_out[c] = (
            part[k, q, tail, :] + c1_in[c, 1 - second_bit].astype(f32)
        ).astype(bf16)
        chain_second(c).start()

    def put(value, start, at):
        count = value.shape[0]
        cut = max(0, min(count, mode_rows - start))
        if cut:
            red_ref[pl.ds(start, cut), at] = value[:cut]
        if cut < count:
            load_ref[pl.ds(start + cut - mode_rows, count - cut), at] = value[cut:]

    def columns_of(c):
        return pl.ds(pl.multiple_of(c * width, width), width)

    def chain_last(k):
        c = k // high
        _, second_bit, _, _, _, _ = order(c)
        chain_second(c).wait_recv()
        put(
            part[k, low, tail, :]
            + c1_in[c, second_bit].astype(f32)
            + c2_in[c].astype(f32),
            direct,
            columns_of(c),
        )

    def step_of(t, carry):
        for c in range(parts):

            @pl.when(t == c * high)
            def _(c=c):
                products(c)

        for step in range(1, n_panel):
            for piece in range(per_panel):

                @pl.when(t == step * per_panel + piece)
                def _(step=step, piece=piece):
                    owner = lax.rem(panel + step, n_panel)
                    panel_copy(n_panel - step, piece, owner).wait_recv()

        @pl.when(t < total_steps)
        def _():
            c, h = t // high, dest(t)
            first_bit, _, first_weight, second_weight, _, _ = order(c)
            product = jnp.dot(
                lhs[h].reshape(LOW * out_rows, rows),
                kphi[c],
                preferred_element_type=f32,
            )
            part[t] = product.reshape(LOW, out_rows, width)
            for j in range(2):
                q = (1 - first_bit) * first_weight + j * second_weight
                s1_out[t, j] = part[t, q, head, :].astype(bf16)
            first_copy(t).start()

        @pl.when((t >= LAG) & (t < total_steps + LAG))
        def _():
            k = t - LAG
            first_bit, second_bit, first_weight, second_weight, _, _ = order(k // high)
            first_copy(k).wait_recv()
            q = first_bit * first_weight + (1 - second_bit) * second_weight
            s2_out[k] = (
                part[k, q, head, :] + s1_in[k, 1 - second_bit].astype(f32)
            ).astype(bf16)
            second_copy(k).start()

        @pl.when((t >= LAG + 1) & (t < total_steps + LAG + 1))
        def _():
            k = t - LAG - 1
            c, h = k // high, dest(k)
            _, second_bit, _, _, _, _ = order(c)
            second_copy(k).wait_recv()
            total = (
                part[k, low, head, :]
                + s1_in[k, second_bit].astype(f32)
                + s2_in[k].astype(f32)
            )

            @pl.when(h != my_high)
            def _():
                z_out[k] = total.astype(bf16)
                third_copy(k, h, c * high + my_high).start()

            @pl.when(h == my_high)
            def _():
                put(total, 0, columns_of(c))

        if chain:

            def hops(i, inner):
                k = t - CHAIN_LAG - i
                inside = (k >= 0) & (k < total_steps)
                h = dest(jnp.maximum(k, 0))
                behind = jnp.where(h > my_high, below, above)
                turn = jnp.where(h == my_high, high - 1, behind)

                @pl.when(inside & (turn == i))
                def _():
                    chain_step(k)

                return inner

            lax.fori_loop(0, high, hops, 0)

            for wait, action in ((2, chain_turn), (3, chain_last)):
                k = t - CHAIN_LAG - (high - 1) - wait

                @pl.when((k >= 0) & (k < total_steps) & (dest(jnp.maximum(k, 0)) == my_high))
                def _(k=k, action=action):
                    action(k)

        return carry

    last = max(LAG + 1, CHAIN_LAG + high - 1 + 3 if chain else 0)
    lax.fori_loop(0, total_steps + last, step_of, 0)

    def gathered(c, carry):
        at = columns_of(c)
        cut = min(direct, mode_rows)

        def one(i, inner):
            slot = c * high + lax.rem(my_high + 1 + i, high)
            third_copy(slot, my_high, slot).wait_recv()
            red_ref[pl.ds(0, cut), at] += z_in[slot, pl.ds(0, cut), :].astype(f32)
            if direct > mode_rows:
                extra = pl.ds(0, direct - mode_rows)
                load_ref[extra, at] += z_in[slot, pl.ds(cut, direct - cut), :].astype(f32)
            return inner

        return lax.fori_loop(0, high - 1, one, carry)

    lax.fori_loop(0, parts, gathered, 0)

    def drained(k, carry):
        first_copy(k).wait_send()
        second_copy(k).wait_send()

        @pl.when(dest(k) != my_high)
        def _():
            third_copy(k, my_high, k).wait_send()
            if chain:
                chain_copy(k, my_high, k).wait_send()

        return carry

    lax.fori_loop(0, total_steps, drained, 0)
    for c in range(parts):
        if chain:
            chain_first(c).wait_send()
            chain_second(c).wait_send()

        @pl.when(sub < n_sub - 1)
        def _(c=c):
            halo_copy(c, 0).wait_send()

        @pl.when(sub > 0)
        def _(c=c):
            halo_copy(c, 1).wait_send()

    for step in range(1, n_panel):
        for piece in range(per_panel):
            panel_copy(step, piece, panel).wait_send()


def body(
    n_sub,
    n_panel,
    stiffness_tiles,
    tile_columns,
    tile_counts,
    phi_modes,
    halo_to_right,
    halo_to_left,
    liner_rows,
    liner_owner,
    liner_slot,
):
    block_rows, slots, tile, _ = stiffness_tiles.shape
    rows, columns = phi_modes.shape
    mode_rows = columns * n_panel // n_sub
    parts, width, high, chain = sizes(n_sub, columns, mode_rows)
    out_rows = mode_rows + IF_DEV
    direct = out_rows - chain
    links = chain or 16
    halo = halo_to_right.shape[0]
    listed = liner_rows.shape[0]
    steps = parts * high
    bf16, f32 = jnp.bfloat16, jnp.float32
    smem = pl.BlockSpec(memory_space=pltpu.SMEM)
    vmem = pl.BlockSpec(memory_space=pltpu.VMEM)
    hbm = pl.BlockSpec(memory_space=pl.ANY)
    dma = pltpu.SemaphoreType.DMA
    chains = steps if chain else 1
    arrivals = parts * (high + 1) if chain else 1
    return pl.pallas_call(
        functools.partial(kernel, n_sub, n_panel, parts, chain),
        out_shape=(
            jax.ShapeDtypeStruct((mode_rows, columns), f32),
            jax.ShapeDtypeStruct((IF_DEV, columns), f32),
        ),
        in_specs=[smem, smem, smem, smem, vmem, vmem, vmem, hbm, hbm],
        out_specs=(vmem, vmem),
        scratch_shapes=[
            pltpu.VMEM((block_rows + 2 * halo + 1, tile, width), bf16)
            for _ in range(parts)
        ]
        + [
            pltpu.VMEM((block_rows, slots, tile, tile), bf16),
            pltpu.VMEM((rows, listed), bf16),
            pltpu.VMEM((high, LOW, out_rows, rows), bf16),
            pltpu.VMEM((parts, rows, width), bf16),
            pltpu.VMEM((steps, LOW, out_rows, width), f32),
            pltpu.VMEM((parts, 2, halo, tile, width), bf16),
            pltpu.VMEM((parts, 2, halo, tile, width), bf16),
            pltpu.VMEM((steps, 2, direct, width), bf16),
            pltpu.VMEM((steps, 2, direct, width), bf16),
            pltpu.VMEM((steps, direct, width), bf16),
            pltpu.VMEM((steps, direct, width), bf16),
            pltpu.VMEM((steps, direct, width), bf16),
            pltpu.VMEM((steps, direct, width), bf16),
            pltpu.VMEM((chains, LOW, links, width), bf16),
            pltpu.VMEM((arrivals, LOW, links, width), bf16),
            pltpu.VMEM((parts, 2, links, width), bf16),
            pltpu.VMEM((parts, 2, links, width), bf16),
            pltpu.VMEM((parts, links, width), bf16),
            pltpu.VMEM((parts, links, width), bf16),
            dma((parts + 1,)),
            dma((parts, 2)),
            dma((parts, 2)),
            dma((n_panel, high // n_panel)),
            dma((n_panel, high // n_panel)),
        ]
        + [dma((steps,))] * 6
        + [dma((chains,)), dma((arrivals,))]
        + [dma((parts,))] * 4,
        compiler_params=pltpu.CompilerParams(
            collective_id=0, has_side_effects=True, vmem_limit_bytes=60 << 20
        ),
    )(
        tile_columns.T,
        tile_counts,
        halo_to_right,
        halo_to_left,
        liner_rows.reshape(1, listed),
        liner_owner.reshape(1, listed),
        liner_slot.reshape(1, listed),
        stiffness_tiles,
        phi_modes.reshape(block_rows, tile, columns),
    )


def solution(mesh):
    return jax.shard_map(
        functools.partial(body, mesh.shape["sub"], mesh.shape["panel"]),
        mesh=mesh,
        in_specs=(
            P("sub", None, None, None),
            P("sub", None),
            P("sub", None),
            P("sub", "panel"),
            P("sub"),
            P("sub"),
            P("sub"),
            P("sub", None),
            P("sub"),
        ),
        out_specs=(P("sub", "panel"), P("sub", "panel")),
        check_vma=False,
    )
```

```python
import functools

import jax
import jax.numpy as jnp
from jax import lax
from jax.experimental import pallas as pl
from jax.experimental.pallas import tpu as pltpu
from jax.sharding import PartitionSpec as P

IF_DEV = 32
LOW = 4
LAG = 3
NEXT = 5
REST = 3
TURNS = (1, 3, 6, 8)
CROSS_ROWS = 48
MESH = pl.DeviceIdType.MESH


def sizes(n_sub, n_panel, width):
    parts = max(1, min(4, width // 128))
    high = n_sub // LOW
    cross = CROSS_ROWS if high == 4 and n_panel == 2 else 0
    return parts, width // parts, high, cross


def kernel(n_sub, n_panel, parts, cross, *refs):
    refs = list(refs)

    def take(count):
        taken, refs[:] = refs[:count], refs[count:]
        return taken

    cols_ref, counts_ref, to_right_ref, to_left_ref, rows_ref, owner_ref, slot_ref = take(7)
    tiles_hbm, phi_hbm, red_ref, load_ref = take(4)
    ext = take(parts)
    tiles, hit, lhs, kphi, part, halo_out, halo_in = take(7)
    s1_out, s1_in, s2_out, s2_in, z_out, z_in = take(6)
    b1_out, b1_in, b2_out, b2_in, b3_out, b3_in, b4_out, b4_in = take(8)
    local_sem, halo_send, halo_recv, pan_send, pan_recv = take(5)
    s1_send, s1_recv, s2_send, s2_recv, z_send, z_recv = take(6)
    b1_send, b1_recv, b2_send, b2_recv, b3_send, b3_recv, b4_send, b4_recv = take(8)

    block_rows, slots, tile, _ = tiles.shape
    halo = halo_out.shape[2]
    rows = block_rows * tile
    width = kphi.shape[2]
    high = n_sub // LOW
    mode_rows = red_ref.shape[0]
    out_rows = mode_rows + IF_DEV
    direct = out_rows - cross
    per_panel = high // n_panel
    total_steps = parts * high
    empty = block_rows + 2 * halo
    f32, bf16 = jnp.float32, jnp.bfloat16
    sub = lax.axis_index("sub")
    panel = lax.axis_index("panel")
    low, my_high = lax.rem(sub, LOW), sub // LOW
    bit0, bit1 = lax.rem(low, 2), low // 2
    odd = lax.rem(panel, 2)

    def first_of(t):
        k = lax.rem(t, 4)
        turn = jnp.where(k == 1 + 2 * odd, 1, 0)
        return jnp.where(t >= total_steps - high, jnp.where(lax.rem(k, 2) == 1 - odd, 1, 0), turn)

    def order(first0):
        swap = 1 - first0
        first_bit = (1 - swap) * bit0 + swap * bit1
        second_bit = (1 - swap) * bit1 + swap * bit0
        first_weight, second_weight = 1 + swap, 2 - swap
        first_peer = sub + (1 - 2 * first_bit) * first_weight
        second_peer = sub + (1 - 2 * second_bit) * second_weight
        return first_bit, second_bit, first_weight, second_weight, first_peer, second_peer

    high0, high1 = lax.rem(my_high, 2), my_high // 2

    def flip(mask):
        mask0, mask1 = lax.rem(mask, 2), mask // 2
        return (high0 + mask0 - 2 * high0 * mask0) + 2 * (high1 + mask1 - 2 * high1 * mask1)

    def mask_of(t):
        k = lax.rem(t, high)
        apart = jnp.abs(high1 - panel)
        begin = 2 * jnp.abs(k // 2 - apart) + 1 - lax.rem(k, 2)
        later = 3 - k // 2 - 2 * lax.rem(k, 2)
        return jnp.where(t < high, begin, later)

    def dest(t):
        if cross:
            return flip(mask_of(t))
        k = lax.rem(t, high)
        return lax.rem(k + jnp.where(t < high, panel * per_panel, my_high + 1), high)

    barrier = pltpu.get_barrier_semaphore()

    def greet(place):
        pl.semaphore_signal(barrier, inc=1, device_id=place, device_id_type=MESH)

    greet({"sub": sub + 1 - 2 * bit0, "panel": panel})
    greet({"sub": sub + 2 - 4 * bit1, "panel": panel})

    @pl.when(sub > 0)
    def _():
        greet({"sub": sub - 1, "panel": panel})

    @pl.when(sub < n_sub - 1)
    def _():
        greet({"sub": sub + 1, "panel": panel})

    for step in range(1, n_panel):
        greet({"sub": sub, "panel": lax.rem(panel + step, n_panel)})
    for step in range(1, high):
        greet({"sub": lax.rem(my_high + step, high) * LOW + low, "panel": panel})

    phi_copies = [
        pltpu.make_async_copy(
            phi_hbm.at[:, :, pl.ds(c * width, width)],
            ext[c].at[pl.ds(halo, block_rows)],
            local_sem.at[c],
        )
        for c in range(parts)
    ]
    tile_copy = pltpu.make_async_copy(tiles_hbm, tiles, local_sem.at[parts])
    for copy in phi_copies:
        copy.start()
    tile_copy.start()

    def halo_copy(c, side):
        return pltpu.make_async_remote_copy(
            src_ref=halo_out.at[c, side],
            dst_ref=halo_in.at[c, side],
            send_sem=halo_send.at[c, side],
            recv_sem=halo_recv.at[c, side],
            device_id={"sub": sub + 1 - 2 * side, "panel": panel},
            device_id_type=MESH,
        )

    def prepare_halo(c):
        phi_copies[c].wait()
        for i in range(halo):
            halo_out[c, 0, i] = ext[c][halo + to_right_ref[i]]
            halo_out[c, 1, i] = ext[c][halo + to_left_ref[i]]

    def send_halo(c):
        @pl.when(sub < n_sub - 1)
        def _():
            halo_copy(c, 0).start()

        @pl.when(sub > 0)
        def _():
            halo_copy(c, 1).start()

    prepare_halo(0)
    ends = jnp.where(sub > 0, 1, 0) + jnp.where(sub < n_sub - 1, 1, 0)
    pl.semaphore_wait(barrier, 2 + (n_panel - 1) + (high - 1) + ends)
    send_halo(0)
    for c in range(1, parts):
        prepare_halo(c)

    def panel_copy(step, piece, owner):
        block = lhs.at[owner * per_panel + piece, :, pl.ds(0, mode_rows), :]
        return pltpu.make_async_remote_copy(
            src_ref=block,
            dst_ref=block,
            send_sem=pan_send.at[step, piece],
            recv_sem=pan_recv.at[step, piece],
            device_id={"sub": sub, "panel": lax.rem(panel + step, n_panel)},
            device_id_type=MESH,
        )

    for piece in range(per_panel):

        def transposed(b, carry, piece=piece):
            for q in range(LOW):
                at = (piece * LOW + q) * mode_rows
                lhs[
                    panel * per_panel + piece,
                    q,
                    pl.ds(0, mode_rows),
                    pl.ds(pl.multiple_of(b * tile, tile), tile),
                ] = jnp.transpose(
                    ext[at // width][halo + b, :, pl.ds(at % width, mode_rows)]
                )
            return carry

        lax.fori_loop(0, block_rows, transposed, 0)
        for step in range(1, n_panel):
            panel_copy(step, piece, panel).start()

    listed = rows_ref.shape[1]
    target = owner_ref[...] * IF_DEV + slot_ref[...]
    places = lax.broadcasted_iota(jnp.int32, (n_sub * IF_DEV, listed), 0)
    hit[...] = (places == target).astype(f32).astype(bf16)
    piece_rows = min(512, rows)

    def select(i, carry):
        at = pl.multiple_of(i * piece_rows, piece_rows)
        place = lax.broadcasted_iota(jnp.int32, (piece_rows, listed), 0) + at
        onehot = (place == rows_ref[...]).astype(f32).astype(bf16)
        found = lax.dot_general(
            hit[...],
            onehot,
            (((1,), (1,)), ((), ())),
            preferred_element_type=f32,
        ).astype(bf16)
        lhs[:, :, pl.ds(mode_rows, IF_DEV), pl.ds(at, piece_rows)] = found.reshape(
            high, LOW, IF_DEV, piece_rows
        )
        return carry

    lax.fori_loop(0, rows // piece_rows, select, 0)
    for c in range(parts):
        ext[c][empty] = jnp.zeros((tile, width), bf16)
    tile_copy.wait()

    def products(c):
        for side in range(2):
            there = sub > 0 if side == 0 else sub < n_sub - 1
            place = pl.ds(side * (halo + block_rows), halo)

            @pl.when(there)
            def _(side=side, place=place):
                halo_copy(c, side).wait_recv()
                ext[c][place] = halo_in[c, side]

            @pl.when(jnp.logical_not(there))
            def _(place=place):
                ext[c][place] = jnp.zeros((halo, tile, width), bf16)

        if c + 1 < parts:
            send_halo(c + 1)

        def block_row(b, carry):
            count = counts_ref[0, b]
            left = jnp.concatenate([tiles[b, j] for j in range(slots)], axis=1)
            right = jnp.concatenate(
                [
                    ext[c][jnp.where(j < count, cols_ref[j, b], empty)]
                    for j in range(slots)
                ],
                axis=0,
            )
            kphi[c, pl.ds(pl.multiple_of(b * tile, tile), tile), :] = jnp.dot(
                left, right, preferred_element_type=f32
            ).astype(bf16)
            return carry

        lax.fori_loop(0, block_rows, block_row, 0, unroll=4)

    def first_copy(k):
        return pltpu.make_async_remote_copy(
            src_ref=s1_out.at[k],
            dst_ref=s1_in.at[k],
            send_sem=s1_send.at[k],
            recv_sem=s1_recv.at[k],
            device_id={"sub": order(first_of(k))[4], "panel": panel},
            device_id_type=MESH,
        )

    def second_copy(k):
        return pltpu.make_async_remote_copy(
            src_ref=s2_out.at[k],
            dst_ref=s2_in.at[k],
            send_sem=s2_send.at[k],
            recv_sem=s2_recv.at[k],
            device_id={"sub": order(first_of(k))[5], "panel": panel},
            device_id_type=MESH,
        )

    def third_copy(k, h, slot):
        return pltpu.make_async_remote_copy(
            src_ref=z_out.at[k],
            dst_ref=z_in.at[slot],
            send_sem=z_send.at[k],
            recv_sem=z_recv.at[slot],
            device_id={"sub": h * LOW + low, "panel": panel},
            device_id_type=MESH,
        )

    def cross_copy(stage, k, place):
        out, into, send, recv = (
            (b1_out, b1_in, b1_send, b1_recv),
            (b2_out, b2_in, b2_send, b2_recv),
            (b3_out, b3_in, b3_send, b3_recv),
            (b4_out, b4_in, b4_send, b4_recv),
        )[stage]
        return pltpu.make_async_remote_copy(
            src_ref=out.at[k],
            dst_ref=into.at[k],
            send_sem=send.at[k],
            recv_sem=recv.at[k],
            device_id={"sub": place, "panel": panel},
            device_id_type=MESH,
        )

    def cross_near(k):
        return cross_copy(0, k, flip(1) * LOW + low)

    def cross_far(c):
        return cross_copy(1, c, flip(2) * LOW + low)

    def cross_first(c):
        return cross_copy(2, c, order(1 - odd)[4])

    def cross_second(c):
        return cross_copy(3, c, order(1 - odd)[5])

    head, tail = pl.ds(0, direct), pl.ds(direct, cross)

    def cross_send(k):
        c = k // high
        at = 2 * c + mask_of(k) // 2
        b1_out[at] = part[k, :, tail, :].astype(bf16)
        cross_near(at).start()

    def cross_pass(k):
        c = k // high
        cross_near(2 * c + 1).wait_recv()
        b2_out[c] = (part[k, :, tail, :] + b1_in[2 * c + 1].astype(f32)).astype(bf16)
        cross_far(c).start()

    def cross_own(k):
        c = k // high
        cross_near(2 * c).wait_recv()
        cross_far(c).wait_recv()
        part[k, :, tail, :] += b1_in[2 * c].astype(f32) + b2_in[c].astype(f32)
        first_bit, _, first_weight, second_weight, _, _ = order(1 - odd)
        for j in range(2):
            q = (1 - first_bit) * first_weight + j * second_weight
            b3_out[c, j] = part[k, q, tail, :].astype(bf16)
        cross_first(c).start()

    def cross_turn(k):
        c = k // high
        first_bit, second_bit, first_weight, second_weight, _, _ = order(1 - odd)
        cross_first(c).wait_recv()
        q = first_bit * first_weight + (1 - second_bit) * second_weight
        b4_out[c] = (
            part[k, q, tail, :] + b3_in[c, 1 - second_bit].astype(f32)
        ).astype(bf16)
        cross_second(c).start()

    def put(value, start, at):
        count = value.shape[0]
        cut = max(0, min(count, mode_rows - start))
        if cut:
            red_ref[pl.ds(start, cut), at] = value[:cut]
        if cut < count:
            load_ref[pl.ds(start + cut - mode_rows, count - cut), at] = value[cut:]

    def columns_of(c):
        return pl.ds(pl.multiple_of(c * width, width), width)

    def cross_last(k):
        c = k // high
        _, second_bit, _, _, _, _ = order(1 - odd)
        cross_second(c).wait_recv()
        put(
            part[k, low, tail, :]
            + b3_in[c, second_bit].astype(f32)
            + b4_in[c].astype(f32),
            direct,
            columns_of(c),
        )

    def gathered(c):
        at = columns_of(c)
        cut = min(direct, mode_rows)

        def one(i, inner):
            slot = c * high + lax.rem(my_high + 1 + i, high)
            third_copy(slot, my_high, slot).wait_recv()
            red_ref[pl.ds(0, cut), at] += z_in[slot, pl.ds(0, cut), :].astype(f32)
            if direct > mode_rows:
                extra = pl.ds(0, direct - mode_rows)
                load_ref[extra, at] += z_in[slot, pl.ds(cut, direct - cut), :].astype(f32)
            return inner

        lax.fori_loop(0, high - 1, one, 0)

    def step_of(t, carry):
        for c in range(parts):

            @pl.when(t == c * high)
            def _(c=c):
                products(c)

        for step in range(1, n_panel):

            @pl.when(t == step * per_panel)
            def _(step=step):
                owner = lax.rem(panel + step, n_panel)
                for piece in range(per_panel):
                    panel_copy(n_panel - step, piece, owner).wait_recv()

        @pl.when(t < total_steps)
        def _():
            c, h = t // high, dest(t)
            first_bit, _, first_weight, second_weight, _, _ = order(first_of(t))
            product = jnp.dot(
                lhs[h].reshape(LOW * out_rows, rows),
                kphi[c],
                preferred_element_type=f32,
            )
            part[t] = product.reshape(LOW, out_rows, width)
            for j in range(2):
                q = (1 - first_bit) * first_weight + j * second_weight
                s1_out[t, j] = part[t, q, head, :].astype(bf16)
            first_copy(t).start()
            if cross:

                @pl.when(lax.rem(mask_of(t), 2) == 1)
                def _():
                    cross_send(t)

        @pl.when((t >= LAG) & (t < total_steps + LAG))
        def _():
            k = t - LAG
            first_bit, second_bit, first_weight, second_weight, _, _ = order(first_of(k))
            first_copy(k).wait_recv()
            q = first_bit * first_weight + (1 - second_bit) * second_weight
            s2_out[k] = (
                part[k, q, head, :] + s1_in[k, 1 - second_bit].astype(f32)
            ).astype(bf16)
            second_copy(k).start()

        @pl.when((t >= NEXT) & (t < total_steps + NEXT))
        def _():
            k = t - NEXT
            c, h = k // high, dest(k)
            _, second_bit, _, _, _, _ = order(first_of(k))
            second_copy(k).wait_recv()
            total = (
                part[k, low, head, :]
                + s1_in[k, second_bit].astype(f32)
                + s2_in[k].astype(f32)
            )

            @pl.when(h != my_high)
            def _():
                z_out[k] = total.astype(bf16)
                third_copy(k, h, c * high + my_high).start()

            @pl.when(h == my_high)
            def _():
                put(total, 0, columns_of(c))

        if cross:
            for wait, mask, action in zip(
                TURNS, (2, 0, 0, 0), (cross_pass, cross_own, cross_turn, cross_last)
            ):
                k = t - wait

                @pl.when((k >= 0) & (k < total_steps) & (mask_of(jnp.maximum(k, 0)) == mask))
                def _(k=k, action=action):
                    action(k)

        done = t - NEXT - REST - (high - 1)

        @pl.when((done >= 0) & (lax.rem(jnp.maximum(done, 0), high) == 0))
        def _():
            gathered(done // high)

        return carry

    last = max(NEXT + REST, TURNS[-1] if cross else 0)
    lax.fori_loop(0, total_steps + last, step_of, 0)

    def drained(k, carry):
        first_copy(k).wait_send()
        second_copy(k).wait_send()

        @pl.when(dest(k) != my_high)
        def _():
            third_copy(k, my_high, k).wait_send()

        return carry

    lax.fori_loop(0, total_steps, drained, 0)
    for c in range(parts):
        if cross:
            cross_near(2 * c).wait_send()
            cross_near(2 * c + 1).wait_send()
            cross_far(c).wait_send()
            cross_first(c).wait_send()
            cross_second(c).wait_send()

        @pl.when(sub < n_sub - 1)
        def _(c=c):
            halo_copy(c, 0).wait_send()

        @pl.when(sub > 0)
        def _(c=c):
            halo_copy(c, 1).wait_send()

    for step in range(1, n_panel):
        for piece in range(per_panel):
            panel_copy(step, piece, panel).wait_send()


def hand_over(red_in, load_in, red_out, load_out):
    red_out[...] = red_in[...]
    load_out[...] = load_in[...]


def body(
    n_sub,
    n_panel,
    stiffness_tiles,
    tile_columns,
    tile_counts,
    phi_modes,
    halo_to_right,
    halo_to_left,
    liner_rows,
    liner_owner,
    liner_slot,
):
    block_rows, slots, tile, _ = stiffness_tiles.shape
    rows, columns = phi_modes.shape
    mode_rows = columns * n_panel // n_sub
    parts, width, high, cross = sizes(n_sub, n_panel, columns)
    out_rows = mode_rows + IF_DEV
    direct = out_rows - cross
    over = cross or 16
    halo = halo_to_right.shape[0]
    listed = liner_rows.shape[0]
    steps = parts * high
    bf16, f32 = jnp.bfloat16, jnp.float32
    smem = pl.BlockSpec(memory_space=pltpu.SMEM)
    vmem = pl.BlockSpec(memory_space=pltpu.VMEM)
    hbm = pl.BlockSpec(memory_space=pl.ANY)
    dma = pltpu.SemaphoreType.DMA
    sums = pl.pallas_call(
        functools.partial(kernel, n_sub, n_panel, parts, cross),
        out_shape=(
            jax.ShapeDtypeStruct((mode_rows, columns), f32),
            jax.ShapeDtypeStruct((IF_DEV, columns), f32),
        ),
        in_specs=[smem, smem, smem, smem, vmem, vmem, vmem, hbm, hbm],
        out_specs=(vmem, vmem),
        scratch_shapes=[
            pltpu.VMEM((block_rows + 2 * halo + 1, tile, width), bf16)
            for _ in range(parts)
        ]
        + [
            pltpu.VMEM((block_rows, slots, tile, tile), bf16),
            pltpu.VMEM((n_sub * IF_DEV, listed), bf16),
            pltpu.VMEM((high, LOW, out_rows, rows), bf16),
            pltpu.VMEM((parts, rows, width), bf16),
            pltpu.VMEM((steps, LOW, out_rows, width), f32),
            pltpu.VMEM((parts, 2, halo, tile, width), bf16),
            pltpu.VMEM((parts, 2, halo, tile, width), bf16),
            pltpu.VMEM((steps, 2, direct, width), bf16),
            pltpu.VMEM((steps, 2, direct, width), bf16),
            pltpu.VMEM((steps, direct, width), bf16),
            pltpu.VMEM((steps, direct, width), bf16),
            pltpu.VMEM((steps, direct, width), bf16),
            pltpu.VMEM((steps, direct, width), bf16),
            pltpu.VMEM((2 * parts, LOW, over, width), bf16),
            pltpu.VMEM((2 * parts, LOW, over, width), bf16),
            pltpu.VMEM((parts, LOW, over, width), bf16),
            pltpu.VMEM((parts, LOW, over, width), bf16),
            pltpu.VMEM((parts, 2, over, width), bf16),
            pltpu.VMEM((parts, 2, over, width), bf16),
            pltpu.VMEM((parts, over, width), bf16),
            pltpu.VMEM((parts, over, width), bf16),
            dma((parts + 1,)),
            dma((parts, 2)),
            dma((parts, 2)),
            dma((n_panel, high // n_panel)),
            dma((n_panel, high // n_panel)),
        ]
        + [dma((steps,))] * 6
        + [dma((2 * parts,))] * 2
        + [dma((parts,))] * 6,
        compiler_params=pltpu.CompilerParams(
            collective_id=0, has_side_effects=True, vmem_limit_bytes=60 << 20
        ),
    )(
        tile_columns.T,
        tile_counts,
        halo_to_right,
        halo_to_left,
        liner_rows.reshape(1, listed),
        liner_owner.reshape(1, listed),
        liner_slot.reshape(1, listed),
        stiffness_tiles,
        phi_modes.reshape(block_rows, tile, columns),
    )
    return pl.pallas_call(
        hand_over,
        out_shape=tuple(jax.ShapeDtypeStruct(x.shape, f32) for x in sums),
        in_specs=[vmem, vmem],
        out_specs=(vmem, vmem),
    )(*sums)


def solution(mesh):
    return jax.shard_map(
        functools.partial(body, mesh.shape["sub"], mesh.shape["panel"]),
        mesh=mesh,
        in_specs=(
            P("sub", None, None, None),
            P("sub", None),
            P("sub", None),
            P("sub", "panel"),
            P("sub"),
            P("sub"),
            P("sub"),
            P("sub", None),
            P("sub"),
        ),
        out_specs=(P("sub", "panel"), P("sub", "panel")),
        check_vma=False,
    )
```

```python
import functools

import jax
import jax.numpy as jnp
from jax import lax
from jax.experimental import pallas as pl
from jax.experimental.pallas import tpu as pltpu
from jax.sharding import PartitionSpec as P

IF_DEV = 32
LOW = 4
LAG = 3
NEXT = 7
REST = 3
TURNS = (1, 3, 7, 10)
CROSS_ROWS = 48
MESH = pl.DeviceIdType.MESH


def sizes(n_sub, n_panel, width):
    parts = max(1, min(4, width // 128))
    high = n_sub // LOW
    cross = CROSS_ROWS if high == 4 and n_panel == 2 else 0
    return parts, width // parts, high, cross


def kernel(n_sub, n_panel, parts, cross, *refs):
    refs = list(refs)

    def take(count):
        taken, refs[:] = refs[:count], refs[count:]
        return taken

    cols_ref, counts_ref, to_right_ref, to_left_ref, rows_ref, owner_ref, slot_ref = take(7)
    tiles_hbm, phi_hbm, red_ref, load_ref = take(4)
    ext = take(parts)
    tiles, hit, lhs, kphi, part, halo_out, halo_in = take(7)
    s1_out, s1_in, s2_out, s2_in, z_out, z_in = take(6)
    b1_out, b1_in, b2_out, b2_in, b3_out, b3_in, b4_out, b4_in = take(8)
    local_sem, halo_send, halo_recv, pan_send, pan_recv = take(5)
    s1_send, s1_recv, s2_send, s2_recv, z_send, z_recv = take(6)
    b1_send, b1_recv, b2_send, b2_recv, b3_send, b3_recv, b4_send, b4_recv = take(8)

    block_rows, slots, tile, _ = tiles.shape
    halo = halo_out.shape[2]
    rows = block_rows * tile
    width = kphi.shape[2]
    high = n_sub // LOW
    mode_rows = red_ref.shape[0]
    out_rows = mode_rows + IF_DEV
    direct = out_rows - cross
    per_panel = high // n_panel
    total_steps = parts * high
    empty = block_rows + 2 * halo
    f32, bf16 = jnp.float32, jnp.bfloat16
    sub = lax.axis_index("sub")
    panel = lax.axis_index("panel")
    low, my_high = lax.rem(sub, LOW), sub // LOW
    bit0, bit1 = lax.rem(low, 2), low // 2
    odd = lax.rem(panel, 2)

    def first_of(t):
        k = lax.rem(t, 4)
        turn = jnp.where(k == 1 + 2 * odd, 1, 0)
        return jnp.where(t >= total_steps - high, jnp.where(lax.rem(k, 2) == 1 - odd, 1, 0), turn)

    def order(first0):
        swap = 1 - first0
        first_bit = (1 - swap) * bit0 + swap * bit1
        second_bit = (1 - swap) * bit1 + swap * bit0
        first_weight, second_weight = 1 + swap, 2 - swap
        first_peer = sub + (1 - 2 * first_bit) * first_weight
        second_peer = sub + (1 - 2 * second_bit) * second_weight
        return first_bit, second_bit, first_weight, second_weight, first_peer, second_peer

    high0, high1 = lax.rem(my_high, 2), my_high // 2

    def flip(mask):
        mask0, mask1 = lax.rem(mask, 2), mask // 2
        return (high0 + mask0 - 2 * high0 * mask0) + 2 * (high1 + mask1 - 2 * high1 * mask1)

    def mask_of(t):
        k = lax.rem(t, high)
        apart = jnp.abs(high1 - panel)
        begin = 2 * jnp.abs(k // 2 - apart) + 1 - lax.rem(k, 2)
        later = 3 - k
        return jnp.where(t < high, begin, later)

    def dest(t):
        if cross:
            return flip(mask_of(t))
        k = lax.rem(t, high)
        return lax.rem(k + jnp.where(t < high, panel * per_panel, my_high + 1), high)

    barrier = pltpu.get_barrier_semaphore()

    def greet(place):
        pl.semaphore_signal(barrier, inc=1, device_id=place, device_id_type=MESH)

    greet({"sub": sub + 1 - 2 * bit0, "panel": panel})
    greet({"sub": sub + 2 - 4 * bit1, "panel": panel})

    @pl.when(sub > 0)
    def _():
        greet({"sub": sub - 1, "panel": panel})

    @pl.when(sub < n_sub - 1)
    def _():
        greet({"sub": sub + 1, "panel": panel})

    for step in range(1, n_panel):
        greet({"sub": sub, "panel": lax.rem(panel + step, n_panel)})
    for step in range(1, high):
        greet({"sub": lax.rem(my_high + step, high) * LOW + low, "panel": panel})

    phi_copies = [
        pltpu.make_async_copy(
            phi_hbm.at[:, :, pl.ds(c * width, width)],
            ext[c].at[pl.ds(halo, block_rows)],
            local_sem.at[c],
        )
        for c in range(parts)
    ]
    tile_copy = pltpu.make_async_copy(tiles_hbm, tiles, local_sem.at[parts])
    for copy in phi_copies:
        copy.start()
    tile_copy.start()

    def halo_copy(c, side):
        return pltpu.make_async_remote_copy(
            src_ref=halo_out.at[c, side],
            dst_ref=halo_in.at[c, side],
            send_sem=halo_send.at[c, side],
            recv_sem=halo_recv.at[c, side],
            device_id={"sub": sub + 1 - 2 * side, "panel": panel},
            device_id_type=MESH,
        )

    def prepare_halo(c):
        phi_copies[c].wait()
        for i in range(halo):
            halo_out[c, 0, i] = ext[c][halo + to_right_ref[i]]
            halo_out[c, 1, i] = ext[c][halo + to_left_ref[i]]

    def send_halo(c):
        @pl.when(sub < n_sub - 1)
        def _():
            halo_copy(c, 0).start()

        @pl.when(sub > 0)
        def _():
            halo_copy(c, 1).start()

    prepare_halo(0)
    ends = jnp.where(sub > 0, 1, 0) + jnp.where(sub < n_sub - 1, 1, 0)
    pl.semaphore_wait(barrier, 2 + (n_panel - 1) + (high - 1) + ends)
    send_halo(0)
    for c in range(1, parts):
        prepare_halo(c)

    def panel_copy(step, piece, owner):
        block = lhs.at[owner * per_panel + piece, :, pl.ds(0, mode_rows), :]
        return pltpu.make_async_remote_copy(
            src_ref=block,
            dst_ref=block,
            send_sem=pan_send.at[step, piece],
            recv_sem=pan_recv.at[step, piece],
            device_id={"sub": sub, "panel": lax.rem(panel + step, n_panel)},
            device_id_type=MESH,
        )

    for piece in range(per_panel):

        def transposed(b, carry, piece=piece):
            for q in range(LOW):
                at = (piece * LOW + q) * mode_rows
                lhs[
                    panel * per_panel + piece,
                    q,
                    pl.ds(0, mode_rows),
                    pl.ds(pl.multiple_of(b * tile, tile), tile),
                ] = jnp.transpose(
                    ext[at // width][halo + b, :, pl.ds(at % width, mode_rows)]
                )
            return carry

        lax.fori_loop(0, block_rows, transposed, 0)
        for step in range(1, n_panel):
            panel_copy(step, piece, panel).start()

    listed = rows_ref.shape[1]
    target = owner_ref[...] * IF_DEV + slot_ref[...]
    places = lax.broadcasted_iota(jnp.int32, (n_sub * IF_DEV, listed), 0)
    hit[...] = (places == target).astype(f32).astype(bf16)
    piece_rows = min(512, rows)

    def select(i, carry):
        at = pl.multiple_of(i * piece_rows, piece_rows)
        place = lax.broadcasted_iota(jnp.int32, (piece_rows, listed), 0) + at
        onehot = (place == rows_ref[...]).astype(f32).astype(bf16)
        found = lax.dot_general(
            hit[...],
            onehot,
            (((1,), (1,)), ((), ())),
            preferred_element_type=f32,
        ).astype(bf16)
        lhs[:, :, pl.ds(mode_rows, IF_DEV), pl.ds(at, piece_rows)] = found.reshape(
            high, LOW, IF_DEV, piece_rows
        )
        return carry

    lax.fori_loop(0, rows // piece_rows, select, 0)
    for c in range(parts):
        ext[c][empty] = jnp.zeros((tile, width), bf16)
    tile_copy.wait()

    def products(c):
        for side in range(2):
            there = sub > 0 if side == 0 else sub < n_sub - 1
            place = pl.ds(side * (halo + block_rows), halo)

            @pl.when(there)
            def _(side=side, place=place):
                halo_copy(c, side).wait_recv()
                ext[c][place] = halo_in[c, side]

            @pl.when(jnp.logical_not(there))
            def _(place=place):
                ext[c][place] = jnp.zeros((halo, tile, width), bf16)

        if c + 1 < parts:
            send_halo(c + 1)

        def block_row(b, carry):
            count = counts_ref[0, b]
            left = jnp.concatenate([tiles[b, j] for j in range(slots)], axis=1)
            right = jnp.concatenate(
                [
                    ext[c][jnp.where(j < count, cols_ref[j, b], empty)]
                    for j in range(slots)
                ],
                axis=0,
            )
            kphi[c, pl.ds(pl.multiple_of(b * tile, tile), tile), :] = jnp.dot(
                left, right, preferred_element_type=f32
            ).astype(bf16)
            return carry

        lax.fori_loop(0, block_rows, block_row, 0, unroll=4)

    def first_copy(k):
        return pltpu.make_async_remote_copy(
            src_ref=s1_out.at[k],
            dst_ref=s1_in.at[k],
            send_sem=s1_send.at[k],
            recv_sem=s1_recv.at[k],
            device_id={"sub": order(first_of(k))[4], "panel": panel},
            device_id_type=MESH,
        )

    def second_copy(k):
        return pltpu.make_async_remote_copy(
            src_ref=s2_out.at[k],
            dst_ref=s2_in.at[k],
            send_sem=s2_send.at[k],
            recv_sem=s2_recv.at[k],
            device_id={"sub": order(first_of(k))[5], "panel": panel},
            device_id_type=MESH,
        )

    def third_copy(k, h, slot):
        return pltpu.make_async_remote_copy(
            src_ref=z_out.at[k],
            dst_ref=z_in.at[slot],
            send_sem=z_send.at[k],
            recv_sem=z_recv.at[slot],
            device_id={"sub": h * LOW + low, "panel": panel},
            device_id_type=MESH,
        )

    def cross_copy(stage, k, place):
        out, into, send, recv = (
            (b1_out, b1_in, b1_send, b1_recv),
            (b2_out, b2_in, b2_send, b2_recv),
            (b3_out, b3_in, b3_send, b3_recv),
            (b4_out, b4_in, b4_send, b4_recv),
        )[stage]
        return pltpu.make_async_remote_copy(
            src_ref=out.at[k],
            dst_ref=into.at[k],
            send_sem=send.at[k],
            recv_sem=recv.at[k],
            device_id={"sub": place, "panel": panel},
            device_id_type=MESH,
        )

    def cross_near(k):
        return cross_copy(0, k, flip(1) * LOW + low)

    def cross_far(c):
        return cross_copy(1, c, flip(2) * LOW + low)

    def cross_first(c):
        return cross_copy(2, c, order(1 - odd)[4])

    def cross_second(c):
        return cross_copy(3, c, order(1 - odd)[5])

    head, tail = pl.ds(0, direct), pl.ds(direct, cross)

    def cross_send(k):
        c = k // high
        at = 2 * c + mask_of(k) // 2
        b1_out[at] = part[k, :, tail, :].astype(bf16)
        cross_near(at).start()

    def cross_pass(k):
        c = k // high
        cross_near(2 * c + 1).wait_recv()
        b2_out[c] = (part[k, :, tail, :] + b1_in[2 * c + 1].astype(f32)).astype(bf16)
        cross_far(c).start()

    def cross_own(k):
        c = k // high
        cross_near(2 * c).wait_recv()
        cross_far(c).wait_recv()
        part[k, :, tail, :] += b1_in[2 * c].astype(f32) + b2_in[c].astype(f32)
        first_bit, _, first_weight, second_weight, _, _ = order(1 - odd)
        for j in range(2):
            q = (1 - first_bit) * first_weight + j * second_weight
            b3_out[c, j] = part[k, q, tail, :].astype(bf16)
        cross_first(c).start()

    def cross_turn(k):
        c = k // high
        first_bit, second_bit, first_weight, second_weight, _, _ = order(1 - odd)
        cross_first(c).wait_recv()
        q = first_bit * first_weight + (1 - second_bit) * second_weight
        b4_out[c] = (
            part[k, q, tail, :] + b3_in[c, 1 - second_bit].astype(f32)
        ).astype(bf16)
        cross_second(c).start()

    def put(value, start, at):
        count = value.shape[0]
        cut = max(0, min(count, mode_rows - start))
        if cut:
            red_ref[pl.ds(start, cut), at] = value[:cut]
        if cut < count:
            load_ref[pl.ds(start + cut - mode_rows, count - cut), at] = value[cut:]

    def columns_of(c):
        return pl.ds(pl.multiple_of(c * width, width), width)

    def cross_last(k):
        c = k // high
        _, second_bit, _, _, _, _ = order(1 - odd)
        cross_second(c).wait_recv()
        put(
            part[k, low, tail, :]
            + b3_in[c, second_bit].astype(f32)
            + b4_in[c].astype(f32),
            direct,
            columns_of(c),
        )

    def gathered(c):
        at = columns_of(c)
        cut = min(direct, mode_rows)

        def one(i, inner):
            slot = c * high + lax.rem(my_high + 1 + i, high)
            third_copy(slot, my_high, slot).wait_recv()
            red_ref[pl.ds(0, cut), at] += z_in[slot, pl.ds(0, cut), :].astype(f32)
            if direct > mode_rows:
                extra = pl.ds(0, direct - mode_rows)
                load_ref[extra, at] += z_in[slot, pl.ds(cut, direct - cut), :].astype(f32)
            return inner

        lax.fori_loop(0, high - 1, one, 0)

    def step_of(t, carry):
        for c in range(parts):

            @pl.when(t == c * high)
            def _(c=c):
                products(c)

        for step in range(1, n_panel):

            @pl.when(t == step * per_panel)
            def _(step=step):
                owner = lax.rem(panel + step, n_panel)
                for piece in range(per_panel):
                    panel_copy(n_panel - step, piece, owner).wait_recv()

        @pl.when(t < total_steps)
        def _():
            c, h = t // high, dest(t)
            first_bit, _, first_weight, second_weight, _, _ = order(first_of(t))
            product = jnp.dot(
                lhs[h].reshape(LOW * out_rows, rows),
                kphi[c],
                preferred_element_type=f32,
            )
            part[t] = product.reshape(LOW, out_rows, width)
            for j in range(2):
                q = (1 - first_bit) * first_weight + j * second_weight
                s1_out[t, j] = part[t, q, head, :].astype(bf16)
            first_copy(t).start()
            if cross:

                @pl.when(lax.rem(mask_of(t), 2) == 1)
                def _():
                    cross_send(t)

        @pl.when((t >= LAG) & (t < total_steps + LAG))
        def _():
            k = t - LAG
            first_bit, second_bit, first_weight, second_weight, _, _ = order(first_of(k))
            first_copy(k).wait_recv()
            q = first_bit * first_weight + (1 - second_bit) * second_weight
            s2_out[k] = (
                part[k, q, head, :] + s1_in[k, 1 - second_bit].astype(f32)
            ).astype(bf16)
            second_copy(k).start()

        @pl.when((t >= NEXT) & (t < total_steps + NEXT))
        def _():
            k = t - NEXT
            c, h = k // high, dest(k)
            _, second_bit, _, _, _, _ = order(first_of(k))
            second_copy(k).wait_recv()
            total = (
                part[k, low, head, :]
                + s1_in[k, second_bit].astype(f32)
                + s2_in[k].astype(f32)
            )

            @pl.when(h != my_high)
            def _():
                z_out[k] = total.astype(bf16)
                third_copy(k, h, c * high + my_high).start()

            @pl.when(h == my_high)
            def _():
                put(total, 0, columns_of(c))

        if cross:
            for wait, mask, action in zip(
                TURNS, (2, 0, 0, 0), (cross_pass, cross_own, cross_turn, cross_last)
            ):
                k = t - wait

                @pl.when((k >= 0) & (k < total_steps) & (mask_of(jnp.maximum(k, 0)) == mask))
                def _(k=k, action=action):
                    action(k)

        done = t - NEXT - REST - (high - 1)

        @pl.when((done >= 0) & (lax.rem(jnp.maximum(done, 0), high) == 0))
        def _():
            gathered(done // high)

        return carry

    last = max(NEXT + REST, TURNS[-1] if cross else 0)
    lax.fori_loop(0, total_steps + last, step_of, 0)

    def drained(k, carry):
        first_copy(k).wait_send()
        second_copy(k).wait_send()

        @pl.when(dest(k) != my_high)
        def _():
            third_copy(k, my_high, k).wait_send()

        return carry

    lax.fori_loop(0, total_steps, drained, 0)
    for c in range(parts):
        if cross:
            cross_near(2 * c).wait_send()
            cross_near(2 * c + 1).wait_send()
            cross_far(c).wait_send()
            cross_first(c).wait_send()
            cross_second(c).wait_send()

        @pl.when(sub < n_sub - 1)
        def _(c=c):
            halo_copy(c, 0).wait_send()

        @pl.when(sub > 0)
        def _(c=c):
            halo_copy(c, 1).wait_send()

    for step in range(1, n_panel):
        for piece in range(per_panel):
            panel_copy(step, piece, panel).wait_send()


def hand_over(red_in, load_in, red_out, load_out):
    red_out[...] = red_in[...]
    load_out[...] = load_in[...]


def body(
    n_sub,
    n_panel,
    stiffness_tiles,
    tile_columns,
    tile_counts,
    phi_modes,
    halo_to_right,
    halo_to_left,
    liner_rows,
    liner_owner,
    liner_slot,
):
    block_rows, slots, tile, _ = stiffness_tiles.shape
    rows, columns = phi_modes.shape
    mode_rows = columns * n_panel // n_sub
    parts, width, high, cross = sizes(n_sub, n_panel, columns)
    out_rows = mode_rows + IF_DEV
    direct = out_rows - cross
    over = cross or 16
    halo = halo_to_right.shape[0]
    listed = liner_rows.shape[0]
    steps = parts * high
    bf16, f32 = jnp.bfloat16, jnp.float32
    smem = pl.BlockSpec(memory_space=pltpu.SMEM)
    vmem = pl.BlockSpec(memory_space=pltpu.VMEM)
    hbm = pl.BlockSpec(memory_space=pl.ANY)
    dma = pltpu.SemaphoreType.DMA
    sums = pl.pallas_call(
        functools.partial(kernel, n_sub, n_panel, parts, cross),
        out_shape=(
            jax.ShapeDtypeStruct((mode_rows, columns), f32),
            jax.ShapeDtypeStruct((IF_DEV, columns), f32),
        ),
        in_specs=[smem, smem, smem, smem, vmem, vmem, vmem, hbm, hbm],
        out_specs=(vmem, vmem),
        scratch_shapes=[
            pltpu.VMEM((block_rows + 2 * halo + 1, tile, width), bf16)
            for _ in range(parts)
        ]
        + [
            pltpu.VMEM((block_rows, slots, tile, tile), bf16),
            pltpu.VMEM((n_sub * IF_DEV, listed), bf16),
            pltpu.VMEM((high, LOW, out_rows, rows), bf16),
            pltpu.VMEM((parts, rows, width), bf16),
            pltpu.VMEM((steps, LOW, out_rows, width), f32),
            pltpu.VMEM((parts, 2, halo, tile, width), bf16),
            pltpu.VMEM((parts, 2, halo, tile, width), bf16),
            pltpu.VMEM((steps, 2, direct, width), bf16),
            pltpu.VMEM((steps, 2, direct, width), bf16),
            pltpu.VMEM((steps, direct, width), bf16),
            pltpu.VMEM((steps, direct, width), bf16),
            pltpu.VMEM((steps, direct, width), bf16),
            pltpu.VMEM((steps, direct, width), bf16),
            pltpu.VMEM((2 * parts, LOW, over, width), bf16),
            pltpu.VMEM((2 * parts, LOW, over, width), bf16),
            pltpu.VMEM((parts, LOW, over, width), bf16),
            pltpu.VMEM((parts, LOW, over, width), bf16),
            pltpu.VMEM((parts, 2, over, width), bf16),
            pltpu.VMEM((parts, 2, over, width), bf16),
            pltpu.VMEM((parts, over, width), bf16),
            pltpu.VMEM((parts, over, width), bf16),
            dma((parts + 1,)),
            dma((parts, 2)),
            dma((parts, 2)),
            dma((n_panel, high // n_panel)),
            dma((n_panel, high // n_panel)),
        ]
        + [dma((steps,))] * 6
        + [dma((2 * parts,))] * 2
        + [dma((parts,))] * 6,
        compiler_params=pltpu.CompilerParams(
            collective_id=0, has_side_effects=True, vmem_limit_bytes=60 << 20
        ),
    )(
        tile_columns.T,
        tile_counts,
        halo_to_right,
        halo_to_left,
        liner_rows.reshape(1, listed),
        liner_owner.reshape(1, listed),
        liner_slot.reshape(1, listed),
        stiffness_tiles,
        phi_modes.reshape(block_rows, tile, columns),
    )
    return pl.pallas_call(
        hand_over,
        out_shape=tuple(jax.ShapeDtypeStruct(x.shape, f32) for x in sums),
        in_specs=[vmem, vmem],
        out_specs=(vmem, vmem),
    )(*sums)


def solution(mesh):
    return jax.shard_map(
        functools.partial(body, mesh.shape["sub"], mesh.shape["panel"]),
        mesh=mesh,
        in_specs=(
            P("sub", None, None, None),
            P("sub", None),
            P("sub", None),
            P("sub", "panel"),
            P("sub"),
            P("sub"),
            P("sub"),
            P("sub", None),
            P("sub"),
        ),
        out_specs=(P("sub", "panel"), P("sub", "panel")),
        check_vma=False,
    )
```

```python
import functools

import jax
import jax.numpy as jnp
from jax import lax
from jax.experimental import pallas as pl
from jax.experimental.pallas import tpu as pltpu
from jax.sharding import PartitionSpec as P

IF_DEV = 32
LOW = 4
LAG = 3
NEXT = 7
REST = 4
TURNS = (1, 3, 7, 10)
CROSS_ROWS = 48
MESH = pl.DeviceIdType.MESH


def sizes(n_sub, n_panel, width):
    parts = max(1, min(4, width // 128))
    high = n_sub // LOW
    cross = CROSS_ROWS if high == 4 and n_panel == 2 else 0
    return parts, width // parts, high, cross


def kernel(n_sub, n_panel, parts, cross, *refs):
    refs = list(refs)

    def take(count):
        taken, refs[:] = refs[:count], refs[count:]
        return taken

    cols_ref, counts_ref, to_right_ref, to_left_ref, rows_ref, owner_ref, slot_ref = take(7)
    tiles_hbm, phi_hbm, red_ref, load_ref = take(4)
    ext = take(parts)
    tiles, hit, lhs, kphi, part, halo_out, halo_in = take(7)
    s1_out, s1_in, s2_out, s2_in, z_out, z_in = take(6)
    b1_out, b1_in, b2_out, b2_in, b3_out, b3_in, b4_out, b4_in = take(8)
    local_sem, halo_send, halo_recv, pan_send, pan_recv = take(5)
    s1_send, s1_recv, s2_send, s2_recv, z_send, z_recv = take(6)
    b1_send, b1_recv, b2_send, b2_recv, b3_send, b3_recv, b4_send, b4_recv = take(8)

    block_rows, slots, tile, _ = tiles.shape
    halo = halo_out.shape[2]
    rows = block_rows * tile
    width = kphi.shape[2]
    high = n_sub // LOW
    mode_rows = red_ref.shape[0]
    out_rows = mode_rows + IF_DEV
    direct = out_rows - cross
    per_panel = high // n_panel
    total_steps = parts * high
    empty = block_rows + 2 * halo
    f32, bf16 = jnp.float32, jnp.bfloat16
    sub = lax.axis_index("sub")
    panel = lax.axis_index("panel")
    low, my_high = lax.rem(sub, LOW), sub // LOW
    bit0, bit1 = lax.rem(low, 2), low // 2
    odd = lax.rem(panel, 2)

    def first_of(t):
        k = lax.rem(t, 4)
        turn = jnp.where(k == 1 + 2 * odd, 1, 0)
        return jnp.where(t >= total_steps - high, jnp.where(lax.rem(k, 2) == 1 - odd, 1, 0), turn)

    def order(first0):
        swap = 1 - first0
        first_bit = (1 - swap) * bit0 + swap * bit1
        second_bit = (1 - swap) * bit1 + swap * bit0
        first_weight, second_weight = 1 + swap, 2 - swap
        first_peer = sub + (1 - 2 * first_bit) * first_weight
        second_peer = sub + (1 - 2 * second_bit) * second_weight
        return first_bit, second_bit, first_weight, second_weight, first_peer, second_peer

    high0, high1 = lax.rem(my_high, 2), my_high // 2

    def flip(mask):
        mask0, mask1 = lax.rem(mask, 2), mask // 2
        return (high0 + mask0 - 2 * high0 * mask0) + 2 * (high1 + mask1 - 2 * high1 * mask1)

    def mask_of(t):
        k = lax.rem(t, high)
        apart = jnp.abs(high1 - panel)
        begin = 2 * jnp.abs(k // 2 - apart) + 1 - lax.rem(k, 2)
        later = 3 - k
        return jnp.where(t < high, begin, later)

    def dest(t):
        if cross:
            return flip(mask_of(t))
        k = lax.rem(t, high)
        return lax.rem(k + jnp.where(t < high, panel * per_panel, my_high + 1), high)

    barrier = pltpu.get_barrier_semaphore()

    def greet(place):
        pl.semaphore_signal(barrier, inc=1, device_id=place, device_id_type=MESH)

    greet({"sub": sub + 1 - 2 * bit0, "panel": panel})
    greet({"sub": sub + 2 - 4 * bit1, "panel": panel})

    @pl.when(sub > 0)
    def _():
        greet({"sub": sub - 1, "panel": panel})

    @pl.when(sub < n_sub - 1)
    def _():
        greet({"sub": sub + 1, "panel": panel})

    for step in range(1, n_panel):
        greet({"sub": sub, "panel": lax.rem(panel + step, n_panel)})
    for step in range(1, high):
        greet({"sub": lax.rem(my_high + step, high) * LOW + low, "panel": panel})

    phi_copies = [
        pltpu.make_async_copy(
            phi_hbm.at[:, :, pl.ds(c * width, width)],
            ext[c].at[pl.ds(halo, block_rows)],
            local_sem.at[c],
        )
        for c in range(parts)
    ]
    tile_copy = pltpu.make_async_copy(tiles_hbm, tiles, local_sem.at[parts])
    for copy in phi_copies:
        copy.start()
    tile_copy.start()

    def halo_copy(c, side):
        return pltpu.make_async_remote_copy(
            src_ref=halo_out.at[c, side],
            dst_ref=halo_in.at[c, side],
            send_sem=halo_send.at[c, side],
            recv_sem=halo_recv.at[c, side],
            device_id={"sub": sub + 1 - 2 * side, "panel": panel},
            device_id_type=MESH,
        )

    def prepare_halo(c):
        phi_copies[c].wait()
        for i in range(halo):
            halo_out[c, 0, i] = ext[c][halo + to_right_ref[i]]
            halo_out[c, 1, i] = ext[c][halo + to_left_ref[i]]

    def send_halo(c):
        @pl.when(sub < n_sub - 1)
        def _():
            halo_copy(c, 0).start()

        @pl.when(sub > 0)
        def _():
            halo_copy(c, 1).start()

    prepare_halo(0)
    listed = rows_ref.shape[1]
    target = owner_ref[...] * IF_DEV + slot_ref[...]
    places = lax.broadcasted_iota(jnp.int32, (n_sub * IF_DEV, listed), 0)
    hit[...] = (places == target).astype(f32).astype(bf16)
    ends = jnp.where(sub > 0, 1, 0) + jnp.where(sub < n_sub - 1, 1, 0)
    pl.semaphore_wait(barrier, 2 + (n_panel - 1) + (high - 1) + ends)
    send_halo(0)
    for c in range(1, parts):
        prepare_halo(c)

    def panel_copy(step, piece, owner):
        block = lhs.at[owner * per_panel + piece, :, pl.ds(0, mode_rows), :]
        return pltpu.make_async_remote_copy(
            src_ref=block,
            dst_ref=block,
            send_sem=pan_send.at[step, piece],
            recv_sem=pan_recv.at[step, piece],
            device_id={"sub": sub, "panel": lax.rem(panel + step, n_panel)},
            device_id_type=MESH,
        )

    for piece in range(per_panel):

        def transposed(b, carry, piece=piece):
            for q in range(LOW):
                at = (piece * LOW + q) * mode_rows
                lhs[
                    panel * per_panel + piece,
                    q,
                    pl.ds(0, mode_rows),
                    pl.ds(pl.multiple_of(b * tile, tile), tile),
                ] = jnp.transpose(
                    ext[at // width][halo + b, :, pl.ds(at % width, mode_rows)]
                )
            return carry

        lax.fori_loop(0, block_rows, transposed, 0)
        for step in range(1, n_panel):
            panel_copy(step, piece, panel).start()

    piece_rows = min(512, rows)

    def select(i, carry):
        at = pl.multiple_of(i * piece_rows, piece_rows)
        place = lax.broadcasted_iota(jnp.int32, (piece_rows, listed), 0) + at
        onehot = (place == rows_ref[...]).astype(f32).astype(bf16)
        found = lax.dot_general(
            hit[...],
            onehot,
            (((1,), (1,)), ((), ())),
            preferred_element_type=f32,
        ).astype(bf16)
        lhs[:, :, pl.ds(mode_rows, IF_DEV), pl.ds(at, piece_rows)] = found.reshape(
            high, LOW, IF_DEV, piece_rows
        )
        return carry

    lax.fori_loop(0, rows // piece_rows, select, 0)
    for c in range(parts):
        ext[c][empty] = jnp.zeros((tile, width), bf16)
    tile_copy.wait()

    def products(c):
        for side in range(2):
            there = sub > 0 if side == 0 else sub < n_sub - 1
            place = pl.ds(side * (halo + block_rows), halo)

            @pl.when(there)
            def _(side=side, place=place):
                halo_copy(c, side).wait_recv()
                ext[c][place] = halo_in[c, side]

            @pl.when(jnp.logical_not(there))
            def _(place=place):
                ext[c][place] = jnp.zeros((halo, tile, width), bf16)

        if c + 1 < parts:
            send_halo(c + 1)

        def block_row(b, carry):
            count = counts_ref[0, b]
            left = jnp.concatenate([tiles[b, j] for j in range(slots)], axis=1)
            right = jnp.concatenate(
                [
                    ext[c][jnp.where(j < count, cols_ref[j, b], empty)]
                    for j in range(slots)
                ],
                axis=0,
            )
            kphi[c, pl.ds(pl.multiple_of(b * tile, tile), tile), :] = jnp.dot(
                left, right, preferred_element_type=f32
            ).astype(bf16)
            return carry

        lax.fori_loop(0, block_rows, block_row, 0, unroll=4)

    def first_copy(k):
        return pltpu.make_async_remote_copy(
            src_ref=s1_out.at[k],
            dst_ref=s1_in.at[k],
            send_sem=s1_send.at[k],
            recv_sem=s1_recv.at[k],
            device_id={"sub": order(first_of(k))[4], "panel": panel},
            device_id_type=MESH,
        )

    def second_copy(k):
        return pltpu.make_async_remote_copy(
            src_ref=s2_out.at[k],
            dst_ref=s2_in.at[k],
            send_sem=s2_send.at[k],
            recv_sem=s2_recv.at[k],
            device_id={"sub": order(first_of(k))[5], "panel": panel},
            device_id_type=MESH,
        )

    def third_copy(k, h, slot):
        return pltpu.make_async_remote_copy(
            src_ref=z_out.at[k],
            dst_ref=z_in.at[slot],
            send_sem=z_send.at[k],
            recv_sem=z_recv.at[slot],
            device_id={"sub": h * LOW + low, "panel": panel},
            device_id_type=MESH,
        )

    def cross_copy(stage, k, place):
        out, into, send, recv = (
            (b1_out, b1_in, b1_send, b1_recv),
            (b2_out, b2_in, b2_send, b2_recv),
            (b3_out, b3_in, b3_send, b3_recv),
            (b4_out, b4_in, b4_send, b4_recv),
        )[stage]
        return pltpu.make_async_remote_copy(
            src_ref=out.at[k],
            dst_ref=into.at[k],
            send_sem=send.at[k],
            recv_sem=recv.at[k],
            device_id={"sub": place, "panel": panel},
            device_id_type=MESH,
        )

    def cross_near(k):
        return cross_copy(0, k, flip(1) * LOW + low)

    def cross_far(c):
        return cross_copy(1, c, flip(2) * LOW + low)

    def cross_first(c):
        return cross_copy(2, c, order(1 - odd)[4])

    def cross_second(c):
        return cross_copy(3, c, order(1 - odd)[5])

    head, tail = pl.ds(0, direct), pl.ds(direct, cross)

    def cross_send(k):
        c = k // high
        at = 2 * c + mask_of(k) // 2
        b1_out[at] = part[k, :, tail, :].astype(bf16)
        cross_near(at).start()

    def cross_pass(k):
        c = k // high
        cross_near(2 * c + 1).wait_recv()
        b2_out[c] = (part[k, :, tail, :] + b1_in[2 * c + 1].astype(f32)).astype(bf16)
        cross_far(c).start()

    def cross_own(k):
        c = k // high
        cross_near(2 * c).wait_recv()
        cross_far(c).wait_recv()
        part[k, :, tail, :] += b1_in[2 * c].astype(f32) + b2_in[c].astype(f32)
        first_bit, _, first_weight, second_weight, _, _ = order(1 - odd)
        for j in range(2):
            q = (1 - first_bit) * first_weight + j * second_weight
            b3_out[c, j] = part[k, q, tail, :].astype(bf16)
        cross_first(c).start()
        cross_near(2 * c).wait_send()
        cross_near(2 * c + 1).wait_send()

    def cross_turn(k):
        c = k // high
        first_bit, second_bit, first_weight, second_weight, _, _ = order(1 - odd)
        cross_first(c).wait_recv()
        q = first_bit * first_weight + (1 - second_bit) * second_weight
        b4_out[c] = (
            part[k, q, tail, :] + b3_in[c, 1 - second_bit].astype(f32)
        ).astype(bf16)
        cross_second(c).start()
        cross_far(c).wait_send()

    def put(value, start, at):
        count = value.shape[0]
        cut = max(0, min(count, mode_rows - start))
        if cut:
            red_ref[pl.ds(start, cut), at] = value[:cut]
        if cut < count:
            load_ref[pl.ds(start + cut - mode_rows, count - cut), at] = value[cut:]

    def columns_of(c):
        return pl.ds(pl.multiple_of(c * width, width), width)

    def cross_last(k):
        c = k // high
        _, second_bit, _, _, _, _ = order(1 - odd)
        cross_second(c).wait_recv()
        cross_first(c).wait_send()
        put(
            part[k, low, tail, :]
            + b3_in[c, second_bit].astype(f32)
            + b4_in[c].astype(f32),
            direct,
            columns_of(c),
        )

    def gathered(c):
        at = columns_of(c)
        cut = min(direct, mode_rows)

        def one(i, inner):
            slot = c * high + lax.rem(my_high + 1 + i, high)
            third_copy(slot, my_high, slot).wait_recv()
            red_ref[pl.ds(0, cut), at] += z_in[slot, pl.ds(0, cut), :].astype(f32)
            if direct > mode_rows:
                extra = pl.ds(0, direct - mode_rows)
                load_ref[extra, at] += z_in[slot, pl.ds(cut, direct - cut), :].astype(f32)
            return inner

        lax.fori_loop(0, high - 1, one, 0)

        def sent(k, inner):
            @pl.when(dest(k) != my_high)
            def _():
                third_copy(k, my_high, k).wait_send()

            return inner

        lax.fori_loop(c * high, (c + 1) * high, sent, 0)

    def step_of(t, carry):
        for c in range(parts):

            @pl.when(t == c * high)
            def _(c=c):
                products(c)

        for step in range(1, n_panel):

            @pl.when(t == step * per_panel)
            def _(step=step):
                owner = lax.rem(panel + step, n_panel)
                for piece in range(per_panel):
                    panel_copy(n_panel - step, piece, owner).wait_recv()

        @pl.when(t < total_steps)
        def _():
            c, h = t // high, dest(t)
            first_bit, _, first_weight, second_weight, _, _ = order(first_of(t))
            product = jnp.dot(
                lhs[h].reshape(LOW * out_rows, rows),
                kphi[c],
                preferred_element_type=f32,
            )
            part[t] = product.reshape(LOW, out_rows, width)
            for j in range(2):
                q = (1 - first_bit) * first_weight + j * second_weight
                s1_out[t, j] = part[t, q, head, :].astype(bf16)
            first_copy(t).start()
            if cross:

                @pl.when(lax.rem(mask_of(t), 2) == 1)
                def _():
                    cross_send(t)

        @pl.when((t >= LAG) & (t < total_steps + LAG))
        def _():
            k = t - LAG
            first_bit, second_bit, first_weight, second_weight, _, _ = order(first_of(k))
            first_copy(k).wait_recv()
            q = first_bit * first_weight + (1 - second_bit) * second_weight
            s2_out[k] = (
                part[k, q, head, :] + s1_in[k, 1 - second_bit].astype(f32)
            ).astype(bf16)
            second_copy(k).start()
            first_copy(k).wait_send()

        @pl.when((t >= NEXT) & (t < total_steps + NEXT))
        def _():
            k = t - NEXT
            c, h = k // high, dest(k)
            _, second_bit, _, _, _, _ = order(first_of(k))
            second_copy(k).wait_recv()
            total = (
                part[k, low, head, :]
                + s1_in[k, second_bit].astype(f32)
                + s2_in[k].astype(f32)
            )

            @pl.when(h != my_high)
            def _():
                z_out[k] = total.astype(bf16)
                third_copy(k, h, c * high + my_high).start()

            @pl.when(h == my_high)
            def _():
                put(total, 0, columns_of(c))

            second_copy(k).wait_send()

        if cross:
            for wait, mask, action in zip(
                TURNS, (2, 0, 0, 0), (cross_pass, cross_own, cross_turn, cross_last)
            ):
                k = t - wait

                @pl.when((k >= 0) & (k < total_steps) & (mask_of(jnp.maximum(k, 0)) == mask))
                def _(k=k, action=action):
                    action(k)

        done = t - NEXT - REST - (high - 1)

        @pl.when((done >= 0) & (lax.rem(jnp.maximum(done, 0), high) == 0))
        def _():
            gathered(done // high)

        return carry

    last = max(NEXT + REST, TURNS[-1] if cross else 0)
    lax.fori_loop(0, total_steps + last, step_of, 0)

    for c in range(parts):
        if cross:
            cross_second(c).wait_send()

        @pl.when(sub < n_sub - 1)
        def _(c=c):
            halo_copy(c, 0).wait_send()

        @pl.when(sub > 0)
        def _(c=c):
            halo_copy(c, 1).wait_send()

    for step in range(1, n_panel):
        for piece in range(per_panel):
            panel_copy(step, piece, panel).wait_send()


def hand_over(red_in, load_in, red_out, load_out):
    red_out[...] = red_in[...]
    load_out[...] = load_in[...]


def body(
    n_sub,
    n_panel,
    stiffness_tiles,
    tile_columns,
    tile_counts,
    phi_modes,
    halo_to_right,
    halo_to_left,
    liner_rows,
    liner_owner,
    liner_slot,
):
    block_rows, slots, tile, _ = stiffness_tiles.shape
    rows, columns = phi_modes.shape
    mode_rows = columns * n_panel // n_sub
    parts, width, high, cross = sizes(n_sub, n_panel, columns)
    out_rows = mode_rows + IF_DEV
    direct = out_rows - cross
    over = cross or 16
    halo = halo_to_right.shape[0]
    listed = liner_rows.shape[0]
    steps = parts * high
    bf16, f32 = jnp.bfloat16, jnp.float32
    smem = pl.BlockSpec(memory_space=pltpu.SMEM)
    vmem = pl.BlockSpec(memory_space=pltpu.VMEM)
    hbm = pl.BlockSpec(memory_space=pl.ANY)
    dma = pltpu.SemaphoreType.DMA
    sums = pl.pallas_call(
        functools.partial(kernel, n_sub, n_panel, parts, cross),
        out_shape=(
            jax.ShapeDtypeStruct((mode_rows, columns), f32),
            jax.ShapeDtypeStruct((IF_DEV, columns), f32),
        ),
        in_specs=[smem, smem, smem, smem, vmem, vmem, vmem, hbm, hbm],
        out_specs=(vmem, vmem),
        scratch_shapes=[
            pltpu.VMEM((block_rows + 2 * halo + 1, tile, width), bf16)
            for _ in range(parts)
        ]
        + [
            pltpu.VMEM((block_rows, slots, tile, tile), bf16),
            pltpu.VMEM((n_sub * IF_DEV, listed), bf16),
            pltpu.VMEM((high, LOW, out_rows, rows), bf16),
            pltpu.VMEM((parts, rows, width), bf16),
            pltpu.VMEM((steps, LOW, out_rows, width), f32),
            pltpu.VMEM((parts, 2, halo, tile, width), bf16),
            pltpu.VMEM((parts, 2, halo, tile, width), bf16),
            pltpu.VMEM((steps, 2, direct, width), bf16),
            pltpu.VMEM((steps, 2, direct, width), bf16),
            pltpu.VMEM((steps, direct, width), bf16),
            pltpu.VMEM((steps, direct, width), bf16),
            pltpu.VMEM((steps, direct, width), bf16),
            pltpu.VMEM((steps, direct, width), bf16),
            pltpu.VMEM((2 * parts, LOW, over, width), bf16),
            pltpu.VMEM((2 * parts, LOW, over, width), bf16),
            pltpu.VMEM((parts, LOW, over, width), bf16),
            pltpu.VMEM((parts, LOW, over, width), bf16),
            pltpu.VMEM((parts, 2, over, width), bf16),
            pltpu.VMEM((parts, 2, over, width), bf16),
            pltpu.VMEM((parts, over, width), bf16),
            pltpu.VMEM((parts, over, width), bf16),
            dma((parts + 1,)),
            dma((parts, 2)),
            dma((parts, 2)),
            dma((n_panel, high // n_panel)),
            dma((n_panel, high // n_panel)),
        ]
        + [dma((steps,))] * 6
        + [dma((2 * parts,))] * 2
        + [dma((parts,))] * 6,
        compiler_params=pltpu.CompilerParams(
            collective_id=0, has_side_effects=True, vmem_limit_bytes=60 << 20
        ),
    )(
        tile_columns.T,
        tile_counts,
        halo_to_right,
        halo_to_left,
        liner_rows.reshape(1, listed),
        liner_owner.reshape(1, listed),
        liner_slot.reshape(1, listed),
        stiffness_tiles,
        phi_modes.reshape(block_rows, tile, columns),
    )
    return pl.pallas_call(
        hand_over,
        out_shape=tuple(jax.ShapeDtypeStruct(x.shape, f32) for x in sums),
        in_specs=[vmem, vmem],
        out_specs=(vmem, vmem),
    )(*sums)


def solution(mesh):
    return jax.shard_map(
        functools.partial(body, mesh.shape["sub"], mesh.shape["panel"]),
        mesh=mesh,
        in_specs=(
            P("sub", None, None, None),
            P("sub", None),
            P("sub", None),
            P("sub", "panel"),
            P("sub"),
            P("sub"),
            P("sub"),
            P("sub", None),
            P("sub"),
        ),
        out_specs=(P("sub", "panel"), P("sub", "panel")),
        check_vma=False,
    )
```

```python
import functools

import jax
import jax.numpy as jnp
from jax import lax
from jax.experimental import pallas as pl
from jax.experimental.pallas import tpu as pltpu
from jax.sharding import PartitionSpec as P

IF_DEV = 32
LOW = 4
LAG = 3
NEXT = 7
REST = 4
TURNS = (1, 3, 7, 10)
CROSS_ROWS = 48
MESH = pl.DeviceIdType.MESH


def sizes(n_sub, n_panel, width):
    parts = max(1, min(4, width // 128))
    high = n_sub // LOW
    cross = CROSS_ROWS if high == 4 and n_panel == 2 else 0
    return parts, width // parts, high, cross


def kernel(n_sub, n_panel, parts, cross, *refs):
    refs = list(refs)

    def take(count):
        taken, refs[:] = refs[:count], refs[count:]
        return taken

    cols_ref, counts_ref, to_right_ref, to_left_ref, rows_ref, owner_ref, slot_ref = take(7)
    tiles_hbm, phi_hbm, red_ref, load_ref = take(4)
    ext = take(parts)
    tiles, hit, lhs, kphi, part, halo_out, halo_in = take(7)
    s1_out, s1_in, s2_out, s2_in, z_out, z_in = take(6)
    b1_out, b1_in, b2_out, b2_in, b3_out, b3_in, b4_out, b4_in = take(8)
    local_sem, halo_send, halo_recv, pan_send, pan_recv = take(5)
    s1_send, s1_recv, s2_send, s2_recv, z_send, z_recv = take(6)
    b1_send, b1_recv, b2_send, b2_recv, b3_send, b3_recv, b4_send, b4_recv = take(8)

    block_rows, slots, tile, _ = tiles.shape
    halo = halo_out.shape[2]
    rows = block_rows * tile
    width = kphi.shape[2]
    high = n_sub // LOW
    mode_rows = red_ref.shape[0]
    out_rows = mode_rows + IF_DEV
    direct = out_rows - cross
    per_panel = high // n_panel
    total_steps = parts * high
    empty = block_rows + 2 * halo
    f32, bf16 = jnp.float32, jnp.bfloat16
    sub = lax.axis_index("sub")
    panel = lax.axis_index("panel")
    low, my_high = lax.rem(sub, LOW), sub // LOW
    bit0, bit1 = lax.rem(low, 2), low // 2
    odd = lax.rem(panel, 2)

    def first_of(t):
        k = lax.rem(t, 4)
        turn = jnp.where(k == 1 + 2 * odd, 1, 0)
        return jnp.where(t >= total_steps - high, jnp.where(lax.rem(k, 2) == 1 - odd, 1, 0), turn)

    def order(first0):
        swap = 1 - first0
        first_bit = (1 - swap) * bit0 + swap * bit1
        second_bit = (1 - swap) * bit1 + swap * bit0
        first_weight, second_weight = 1 + swap, 2 - swap
        first_peer = sub + (1 - 2 * first_bit) * first_weight
        second_peer = sub + (1 - 2 * second_bit) * second_weight
        return first_bit, second_bit, first_weight, second_weight, first_peer, second_peer

    high0, high1 = lax.rem(my_high, 2), my_high // 2

    def flip(mask):
        mask0, mask1 = lax.rem(mask, 2), mask // 2
        return (high0 + mask0 - 2 * high0 * mask0) + 2 * (high1 + mask1 - 2 * high1 * mask1)

    def mask_of(t):
        k = lax.rem(t, high)
        apart = jnp.abs(high1 - panel)
        begin = 2 * jnp.abs(k // 2 - apart) + 1 - lax.rem(k, 2)
        later = 3 - k
        return jnp.where(t < high, begin, later)

    def dest(t):
        if cross:
            return flip(mask_of(t))
        k = lax.rem(t, high)
        return lax.rem(k + jnp.where(t < high, panel * per_panel, my_high + 1), high)

    barrier = pltpu.get_barrier_semaphore()

    def greet(place):
        pl.semaphore_signal(barrier, inc=1, device_id=place, device_id_type=MESH)

    greet({"sub": sub + 1 - 2 * bit0, "panel": panel})
    greet({"sub": sub + 2 - 4 * bit1, "panel": panel})

    @pl.when(sub > 0)
    def _():
        greet({"sub": sub - 1, "panel": panel})

    @pl.when(sub < n_sub - 1)
    def _():
        greet({"sub": sub + 1, "panel": panel})

    for step in range(1, n_panel):
        greet({"sub": sub, "panel": lax.rem(panel + step, n_panel)})
    for step in range(1, high):
        greet({"sub": lax.rem(my_high + step, high) * LOW + low, "panel": panel})

    phi_copies = [
        pltpu.make_async_copy(
            phi_hbm.at[:, :, pl.ds(c * width, width)],
            ext[c].at[pl.ds(halo, block_rows)],
            local_sem.at[c],
        )
        for c in range(parts)
    ]
    tile_copy = pltpu.make_async_copy(tiles_hbm, tiles, local_sem.at[parts])
    for copy in phi_copies:
        copy.start()
    tile_copy.start()

    def halo_copy(c, side):
        return pltpu.make_async_remote_copy(
            src_ref=halo_out.at[c, side],
            dst_ref=halo_in.at[c, side],
            send_sem=halo_send.at[c, side],
            recv_sem=halo_recv.at[c, side],
            device_id={"sub": sub + 1 - 2 * side, "panel": panel},
            device_id_type=MESH,
        )

    def prepare_halo(c):
        phi_copies[c].wait()
        for i in range(halo):
            halo_out[c, 0, i] = ext[c][halo + to_right_ref[i]]
            halo_out[c, 1, i] = ext[c][halo + to_left_ref[i]]

    def send_halo(c):
        @pl.when(sub < n_sub - 1)
        def _():
            halo_copy(c, 0).start()

        @pl.when(sub > 0)
        def _():
            halo_copy(c, 1).start()

    prepare_halo(0)
    listed = rows_ref.shape[1]
    target = owner_ref[...] * IF_DEV + slot_ref[...]
    places = lax.broadcasted_iota(jnp.int32, (n_sub * IF_DEV, listed), 0)
    hit[...] = (places == target).astype(f32).astype(bf16)
    ends = jnp.where(sub > 0, 1, 0) + jnp.where(sub < n_sub - 1, 1, 0)
    pl.semaphore_wait(barrier, 2 + (n_panel - 1) + (high - 1) + ends)
    send_halo(0)
    for c in range(1, parts):
        prepare_halo(c)

    def panel_copy(step, piece, owner):
        block = lhs.at[owner * per_panel + piece, :, pl.ds(0, mode_rows), :]
        return pltpu.make_async_remote_copy(
            src_ref=block,
            dst_ref=block,
            send_sem=pan_send.at[step, piece],
            recv_sem=pan_recv.at[step, piece],
            device_id={"sub": sub, "panel": lax.rem(panel + step, n_panel)},
            device_id_type=MESH,
        )

    for piece in range(per_panel):

        def transposed(b, carry, piece=piece):
            for q in range(LOW):
                at = (piece * LOW + q) * mode_rows
                lhs[
                    panel * per_panel + piece,
                    q,
                    pl.ds(0, mode_rows),
                    pl.ds(pl.multiple_of(b * tile, tile), tile),
                ] = jnp.transpose(
                    ext[at // width][halo + b, :, pl.ds(at % width, mode_rows)]
                )
            return carry

        lax.fori_loop(0, block_rows, transposed, 0)
        for step in range(1, n_panel):
            panel_copy(step, piece, panel).start()

    piece_rows = min(512, rows)

    def select(i, carry):
        at = pl.multiple_of(i * piece_rows, piece_rows)
        place = lax.broadcasted_iota(jnp.int32, (piece_rows, listed), 0) + at
        onehot = (place == rows_ref[...]).astype(f32).astype(bf16)
        found = lax.dot_general(
            hit[...],
            onehot,
            (((1,), (1,)), ((), ())),
            preferred_element_type=f32,
        ).astype(bf16)
        lhs[:, :, pl.ds(mode_rows, IF_DEV), pl.ds(at, piece_rows)] = found.reshape(
            high, LOW, IF_DEV, piece_rows
        )
        return carry

    lax.fori_loop(0, rows // piece_rows, select, 0)
    for c in range(parts):
        ext[c][empty] = jnp.zeros((tile, width), bf16)
    tile_copy.wait()

    def products(c):
        for side in range(2):
            there = sub > 0 if side == 0 else sub < n_sub - 1
            place = pl.ds(side * (halo + block_rows), halo)

            @pl.when(there)
            def _(side=side, place=place):
                halo_copy(c, side).wait_recv()
                ext[c][place] = halo_in[c, side]

            @pl.when(jnp.logical_not(there))
            def _(place=place):
                ext[c][place] = jnp.zeros((halo, tile, width), bf16)

        if c + 1 < parts:
            send_halo(c + 1)

        def block_row(b, carry):
            count = counts_ref[0, b]
            left = jnp.concatenate([tiles[b, j] for j in range(slots)], axis=1)
            right = jnp.concatenate(
                [
                    ext[c][jnp.where(j < count, cols_ref[j, b], empty)]
                    for j in range(slots)
                ],
                axis=0,
            )
            kphi[c, pl.ds(pl.multiple_of(b * tile, tile), tile), :] = jnp.dot(
                left, right, preferred_element_type=f32
            ).astype(bf16)
            return carry

        lax.fori_loop(0, block_rows, block_row, 0, unroll=16)

    def first_copy(k):
        return pltpu.make_async_remote_copy(
            src_ref=s1_out.at[k],
            dst_ref=s1_in.at[k],
            send_sem=s1_send.at[k],
            recv_sem=s1_recv.at[k],
            device_id={"sub": order(first_of(k))[4], "panel": panel},
            device_id_type=MESH,
        )

    def second_copy(k):
        return pltpu.make_async_remote_copy(
            src_ref=s2_out.at[k],
            dst_ref=s2_in.at[k],
            send_sem=s2_send.at[k],
            recv_sem=s2_recv.at[k],
            device_id={"sub": order(first_of(k))[5], "panel": panel},
            device_id_type=MESH,
        )

    def third_copy(k, h, slot):
        return pltpu.make_async_remote_copy(
            src_ref=z_out.at[k],
            dst_ref=z_in.at[slot],
            send_sem=z_send.at[k],
            recv_sem=z_recv.at[slot],
            device_id={"sub": h * LOW + low, "panel": panel},
            device_id_type=MESH,
        )

    def cross_copy(stage, k, place):
        out, into, send, recv = (
            (b1_out, b1_in, b1_send, b1_recv),
            (b2_out, b2_in, b2_send, b2_recv),
            (b3_out, b3_in, b3_send, b3_recv),
            (b4_out, b4_in, b4_send, b4_recv),
        )[stage]
        return pltpu.make_async_remote_copy(
            src_ref=out.at[k],
            dst_ref=into.at[k],
            send_sem=send.at[k],
            recv_sem=recv.at[k],
            device_id={"sub": place, "panel": panel},
            device_id_type=MESH,
        )

    def cross_near(k):
        return cross_copy(0, k, flip(1) * LOW + low)

    def cross_far(c):
        return cross_copy(1, c, flip(2) * LOW + low)

    def cross_first(c):
        return cross_copy(2, c, order(1 - odd)[4])

    def cross_second(c):
        return cross_copy(3, c, order(1 - odd)[5])

    head, tail = pl.ds(0, direct), pl.ds(direct, cross)

    def cross_send(k):
        c = k // high
        at = 2 * c + mask_of(k) // 2
        b1_out[at] = part[k, :, tail, :].astype(bf16)
        cross_near(at).start()

    def cross_pass(k):
        c = k // high
        cross_near(2 * c + 1).wait_recv()
        b2_out[c] = (part[k, :, tail, :] + b1_in[2 * c + 1].astype(f32)).astype(bf16)
        cross_far(c).start()

    def cross_own(k):
        c = k // high
        cross_near(2 * c).wait_recv()
        cross_far(c).wait_recv()
        part[k, :, tail, :] += b1_in[2 * c].astype(f32) + b2_in[c].astype(f32)
        first_bit, _, first_weight, second_weight, _, _ = order(1 - odd)
        for j in range(2):
            q = (1 - first_bit) * first_weight + j * second_weight
            b3_out[c, j] = part[k, q, tail, :].astype(bf16)
        cross_first(c).start()
        cross_near(2 * c).wait_send()
        cross_near(2 * c + 1).wait_send()

    def cross_turn(k):
        c = k // high
        first_bit, second_bit, first_weight, second_weight, _, _ = order(1 - odd)
        cross_first(c).wait_recv()
        q = first_bit * first_weight + (1 - second_bit) * second_weight
        b4_out[c] = (
            part[k, q, tail, :] + b3_in[c, 1 - second_bit].astype(f32)
        ).astype(bf16)
        cross_second(c).start()
        cross_far(c).wait_send()

    def put(value, start, at):
        count = value.shape[0]
        cut = max(0, min(count, mode_rows - start))
        if cut:
            red_ref[pl.ds(start, cut), at] = value[:cut]
        if cut < count:
            load_ref[pl.ds(start + cut - mode_rows, count - cut), at] = value[cut:]

    def columns_of(c):
        return pl.ds(pl.multiple_of(c * width, width), width)

    def cross_last(k):
        c = k // high
        _, second_bit, _, _, _, _ = order(1 - odd)
        cross_second(c).wait_recv()
        cross_first(c).wait_send()
        put(
            part[k, low, tail, :]
            + b3_in[c, second_bit].astype(f32)
            + b4_in[c].astype(f32),
            direct,
            columns_of(c),
        )

    def gathered(c):
        at = columns_of(c)
        cut = min(direct, mode_rows)

        def one(i, inner):
            slot = c * high + lax.rem(my_high + 1 + i, high)
            third_copy(slot, my_high, slot).wait_recv()
            red_ref[pl.ds(0, cut), at] += z_in[slot, pl.ds(0, cut), :].astype(f32)
            if direct > mode_rows:
                extra = pl.ds(0, direct - mode_rows)
                load_ref[extra, at] += z_in[slot, pl.ds(cut, direct - cut), :].astype(f32)
            return inner

        lax.fori_loop(0, high - 1, one, 0)

        def sent(k, inner):
            @pl.when(dest(k) != my_high)
            def _():
                third_copy(k, my_high, k).wait_send()

            return inner

        lax.fori_loop(c * high, (c + 1) * high, sent, 0)

    def step_of(t, carry):
        for c in range(parts):

            @pl.when(t == c * high)
            def _(c=c):
                products(c)

        for step in range(1, n_panel):

            @pl.when(t == step * per_panel)
            def _(step=step):
                owner = lax.rem(panel + step, n_panel)
                for piece in range(per_panel):
                    panel_copy(n_panel - step, piece, owner).wait_recv()

        @pl.when(t < total_steps)
        def _():
            c, h = t // high, dest(t)
            first_bit, _, first_weight, second_weight, _, _ = order(first_of(t))
            product = jnp.dot(
                lhs[h].reshape(LOW * out_rows, rows),
                kphi[c],
                preferred_element_type=f32,
            )
            part[t] = product.reshape(LOW, out_rows, width)
            for j in range(2):
                q = (1 - first_bit) * first_weight + j * second_weight
                s1_out[t, j] = part[t, q, head, :].astype(bf16)
            first_copy(t).start()
            if cross:

                @pl.when(lax.rem(mask_of(t), 2) == 1)
                def _():
                    cross_send(t)

        @pl.when((t >= LAG) & (t < total_steps + LAG))
        def _():
            k = t - LAG
            first_bit, second_bit, first_weight, second_weight, _, _ = order(first_of(k))
            first_copy(k).wait_recv()
            q = first_bit * first_weight + (1 - second_bit) * second_weight
            s2_out[k] = (
                part[k, q, head, :] + s1_in[k, 1 - second_bit].astype(f32)
            ).astype(bf16)
            second_copy(k).start()
            first_copy(k).wait_send()

        @pl.when((t >= NEXT) & (t < total_steps + NEXT))
        def _():
            k = t - NEXT
            c, h = k // high, dest(k)
            _, second_bit, _, _, _, _ = order(first_of(k))
            second_copy(k).wait_recv()
            total = (
                part[k, low, head, :]
                + s1_in[k, second_bit].astype(f32)
                + s2_in[k].astype(f32)
            )

            @pl.when(h != my_high)
            def _():
                z_out[k] = total.astype(bf16)
                third_copy(k, h, c * high + my_high).start()

            @pl.when(h == my_high)
            def _():
                put(total, 0, columns_of(c))

            second_copy(k).wait_send()

        if cross:
            for wait, mask, action in zip(
                TURNS, (2, 0, 0, 0), (cross_pass, cross_own, cross_turn, cross_last)
            ):
                k = t - wait

                @pl.when((k >= 0) & (k < total_steps) & (mask_of(jnp.maximum(k, 0)) == mask))
                def _(k=k, action=action):
                    action(k)

        done = t - NEXT - REST - (high - 1)

        @pl.when((done >= 0) & (lax.rem(jnp.maximum(done, 0), high) == 0))
        def _():
            gathered(done // high)

        return carry

    last = max(NEXT + REST, TURNS[-1] if cross else 0)
    lax.fori_loop(0, total_steps + last, step_of, 0)

    for c in range(parts):
        if cross:
            cross_second(c).wait_send()

        @pl.when(sub < n_sub - 1)
        def _(c=c):
            halo_copy(c, 0).wait_send()

        @pl.when(sub > 0)
        def _(c=c):
            halo_copy(c, 1).wait_send()

    for step in range(1, n_panel):
        for piece in range(per_panel):
            panel_copy(step, piece, panel).wait_send()


def hand_over(red_in, load_in, red_out, load_out):
    red_out[...] = red_in[...]
    load_out[...] = load_in[...]


def body(
    n_sub,
    n_panel,
    stiffness_tiles,
    tile_columns,
    tile_counts,
    phi_modes,
    halo_to_right,
    halo_to_left,
    liner_rows,
    liner_owner,
    liner_slot,
):
    block_rows, slots, tile, _ = stiffness_tiles.shape
    rows, columns = phi_modes.shape
    mode_rows = columns * n_panel // n_sub
    parts, width, high, cross = sizes(n_sub, n_panel, columns)
    out_rows = mode_rows + IF_DEV
    direct = out_rows - cross
    over = cross or 16
    halo = halo_to_right.shape[0]
    listed = liner_rows.shape[0]
    steps = parts * high
    bf16, f32 = jnp.bfloat16, jnp.float32
    smem = pl.BlockSpec(memory_space=pltpu.SMEM)
    vmem = pl.BlockSpec(memory_space=pltpu.VMEM)
    hbm = pl.BlockSpec(memory_space=pl.ANY)
    dma = pltpu.SemaphoreType.DMA
    sums = pl.pallas_call(
        functools.partial(kernel, n_sub, n_panel, parts, cross),
        out_shape=(
            jax.ShapeDtypeStruct((mode_rows, columns), f32),
            jax.ShapeDtypeStruct((IF_DEV, columns), f32),
        ),
        in_specs=[smem, smem, smem, smem, vmem, vmem, vmem, hbm, hbm],
        out_specs=(vmem, vmem),
        scratch_shapes=[
            pltpu.VMEM((block_rows + 2 * halo + 1, tile, width), bf16)
            for _ in range(parts)
        ]
        + [
            pltpu.VMEM((block_rows, slots, tile, tile), bf16),
            pltpu.VMEM((n_sub * IF_DEV, listed), bf16),
            pltpu.VMEM((high, LOW, out_rows, rows), bf16),
            pltpu.VMEM((parts, rows, width), bf16),
            pltpu.VMEM((steps, LOW, out_rows, width), f32),
            pltpu.VMEM((parts, 2, halo, tile, width), bf16),
            pltpu.VMEM((parts, 2, halo, tile, width), bf16),
            pltpu.VMEM((steps, 2, direct, width), bf16),
            pltpu.VMEM((steps, 2, direct, width), bf16),
            pltpu.VMEM((steps, direct, width), bf16),
            pltpu.VMEM((steps, direct, width), bf16),
            pltpu.VMEM((steps, direct, width), bf16),
            pltpu.VMEM((steps, direct, width), bf16),
            pltpu.VMEM((2 * parts, LOW, over, width), bf16),
            pltpu.VMEM((2 * parts, LOW, over, width), bf16),
            pltpu.VMEM((parts, LOW, over, width), bf16),
            pltpu.VMEM((parts, LOW, over, width), bf16),
            pltpu.VMEM((parts, 2, over, width), bf16),
            pltpu.VMEM((parts, 2, over, width), bf16),
            pltpu.VMEM((parts, over, width), bf16),
            pltpu.VMEM((parts, over, width), bf16),
            dma((parts + 1,)),
            dma((parts, 2)),
            dma((parts, 2)),
            dma((n_panel, high // n_panel)),
            dma((n_panel, high // n_panel)),
        ]
        + [dma((steps,))] * 6
        + [dma((2 * parts,))] * 2
        + [dma((parts,))] * 6,
        compiler_params=pltpu.CompilerParams(
            collective_id=0, has_side_effects=True, vmem_limit_bytes=60 << 20
        ),
    )(
        tile_columns.T,
        tile_counts,
        halo_to_right,
        halo_to_left,
        liner_rows.reshape(1, listed),
        liner_owner.reshape(1, listed),
        liner_slot.reshape(1, listed),
        stiffness_tiles,
        phi_modes.reshape(block_rows, tile, columns),
    )
    return pl.pallas_call(
        hand_over,
        out_shape=tuple(jax.ShapeDtypeStruct(x.shape, f32) for x in sums),
        in_specs=[vmem, vmem],
        out_specs=(vmem, vmem),
    )(*sums)


def solution(mesh):
    return jax.shard_map(
        functools.partial(body, mesh.shape["sub"], mesh.shape["panel"]),
        mesh=mesh,
        in_specs=(
            P("sub", None, None, None),
            P("sub", None),
            P("sub", None),
            P("sub", "panel"),
            P("sub"),
            P("sub"),
            P("sub"),
            P("sub", None),
            P("sub"),
        ),
        out_specs=(P("sub", "panel"), P("sub", "panel")),
        check_vma=False,
    )
```
